256 devices in a mesh: dp: 32 (over z, y), head: 8 (over x, core).
Axes of the slice: x: 4, y: 4, z: 8, core: 2. Of those that a mesh axis runs over, the one named last changes fastest.
Arguments:
- teacher_feats: bfloat16 [8192, 384], P('dp'), as said below
- student_feats: bfloat16 [8192, 384], P('dp'), as said below
- prototypes: bfloat16 [65536, 384], P(('dp', 'head')), as said below
Outputs:
- proto_grad: float32 [65536, 384], P(('dp', 'head'))
Inputs may be any that keep to these rules, and one draw needn't show every extreme that they name: `teacher_feats`: finite values. `student_feats`: finite values. `prototypes`: finite values.
All inputs are finite; a program needn't handle non-finite values.
Results may differ from the reference program's by a relative error of at most 0.0034.
Values may be sent and summed in bfloat16 or wider, within the bound.
No kernel may reach another device: no remote copies, remote signals or barrier semaphores. Data moves between devices by JAX's collectives and lax.ppermute only.
A program may use at most 128 MiB of HBM per device.

```python
import math
import jax
import jax.numpy as jnp
import numpy as np
from jax import lax

K = 384
PROTO = 65536
ITERS = 3
TOKENS = 8192


rank_bounds = np.cumsum(np.array([4096 // (m + 1) for m in range(32)], dtype=np.int64)).astype(np.int32)


def cluster_ranks(key, count):
    ticket = jax.random.randint(key, (count,), 0, int(rank_bounds[-1]), dtype=jnp.int32)
    bounds = jnp.asarray(rank_bounds[:-1])
    return jnp.sum((ticket[:, None] >= bounds[None, :]).astype(jnp.int32), axis=1)


def shared_layout(key, spread):
    centroids = jax.random.normal(jax.random.fold_in(key, 101), (32, K), jnp.float32)
    column_scale = jnp.exp(spread * jax.random.uniform(jax.random.fold_in(key, 102), (K,), jnp.float32))
    token_order = jax.random.permutation(jax.random.fold_in(key, 103), 32)
    proto_order = jax.random.permutation(jax.random.fold_in(key, 104), 32)
    token_ranks = jnp.sort(cluster_ranks(jax.random.fold_in(key, 105), TOKENS))
    token_cluster = token_order[token_ranks]
    proto_cluster = proto_order[cluster_ranks(jax.random.fold_in(key, 106), PROTO)]
    return (centroids, column_scale, token_cluster, proto_cluster)


def draw_teacher_feats(key, part):
    base_key = key
    key = jax.random.fold_in(key, 1)
    spread = 0.0
    noise = jax.random.normal(key, (TOKENS, K), jnp.float32)
    centroids, column_scale, token_cluster, proto_cluster = shared_layout(base_key, spread)
    values = (centroids[token_cluster] + 1.5 * noise) * column_scale[None, :]
    return values.astype(jnp.bfloat16)


def draw_student_feats(key, part):
    base_key = key
    key = jax.random.fold_in(key, 2)
    spread = 0.0
    noise = jax.random.normal(key, (TOKENS, K), jnp.float32)
    centroids, column_scale, token_cluster, proto_cluster = shared_layout(base_key, spread)
    values = (centroids[token_cluster] + 1.5 * noise) * column_scale[None, :]
    return values.astype(jnp.bfloat16)


def draw_prototypes(key, part):
    base_key = key
    key = jax.random.fold_in(key, 3)
    spread = 0.0
    noise = jax.random.normal(key, (PROTO, K), jnp.float32)
    centroids, column_scale, token_cluster, proto_cluster = shared_layout(base_key, spread)
    values = (centroids[proto_cluster] + 1.5 * noise) * column_scale[None, :] * K ** (-0.5)
    return values.astype(jnp.bfloat16)


def setup_inputs(seed: int = 0) -> dict:
    seeds = jax.random.split(jax.random.key(seed), 4)
    teacher_feats = draw_teacher_feats(jax.random.fold_in(seeds[3], 71), 0)
    student_feats = draw_student_feats(jax.random.fold_in(seeds[3], 71), 0)
    prototypes = draw_prototypes(jax.random.fold_in(seeds[3], 71), 0)
    return {"teacher_feats": teacher_feats, "student_feats": student_feats, "prototypes": prototypes}


temp_teacher = 0.07
temp_student = 0.1

def unit_rows(values):
    wide = values.astype(jnp.float32)
    return (wide * lax.rsqrt(lax.optimization_barrier(jnp.sum(wide * wide, axis=1, keepdims=True)) + 1e-06)).astype(jnp.bfloat16)

def reference(teacher_feats, student_feats, prototypes):
    teach = unit_rows(teacher_feats)
    stud = unit_rows(student_feats)
    protos = unit_rows(prototypes)
    block = math.gcd(TOKENS, 512)
    count = TOKENS // block
    teach_blocks = teach.reshape(count, block, K)
    stud_blocks = stud.reshape(count, block, K)

    def teacher_block(rows_in):
        return jnp.exp(jnp.dot(rows_in, protos.T, preferred_element_type=jnp.float32) / temp_teacher)
    expo = lax.map(teacher_block, teach_blocks).reshape(TOKENS, PROTO)
    weights_r = jnp.ones((TOKENS,), jnp.float32)
    weights_c = jnp.ones((PROTO,), jnp.float32)
    for step in range(ITERS):
        weights_c = 1.0 / jnp.dot(weights_r, expo, precision=lax.Precision.HIGHEST)
        weights_r = 1.0 / jnp.dot(expo, weights_c, precision=lax.Precision.HIGHEST)
    scale = PROTO / (temp_student * math.sqrt(TOKENS))
    expo_blocks = expo.reshape(count, block, PROTO)
    r_blocks = weights_r.reshape(count, block)

    def grad_step(total, items):
        stud_blk, expo_blk, r_blk = items
        logits = jnp.dot(stud_blk, protos.T, preferred_element_type=jnp.float32) / temp_student
        expz = jnp.exp(logits)
        probs = expz / lax.optimization_barrier(jnp.sum(expz, axis=1, keepdims=True))
        targets = expo_blk * weights_c[None, :] * r_blk[:, None]
        grads = (scale * (probs - targets)).astype(jnp.bfloat16)
        return (total + jnp.dot(grads.T, stud_blk, preferred_element_type=jnp.float32), None)
    total, unused = lax.scan(grad_step, jnp.zeros((PROTO, K), jnp.float32), (stud_blocks, expo_blocks, r_blocks))
    return total
```

```python
import functools
import math

import jax
import jax.numpy as jnp
from jax import lax
from jax.experimental import pallas as pl
from jax.experimental.pallas import tpu as pltpu
from jax.sharding import Mesh, PartitionSpec as P

K = 384
PROTO = 65536
TOKENS = 8192
ITERS = 3
TEMP_TEACHER = 0.07
TEMP_STUDENT = 0.1
LOG2E = math.log2(math.e)
SCALE = PROTO / (TEMP_STUDENT * math.sqrt(TOKENS))

NZ, NY, NX, NC = 8, 4, 4, 2
TOK_BLOCK = TOKENS // (NZ * NY)
TOK_HALF = TOK_BLOCK // NC
PRO_BLOCK = PROTO // (NZ * NY * NX * NC)
TOK = TOK_HALF * NZ
PRO = PRO_BLOCK * NY * NC
HALF = PRO // 2
LANES = 128
TROWS = TOK // LANES
PROWS = PRO // LANES
TGROUP = NY * NC
PGROUP = NZ * NX

F32 = jnp.float32
BF16 = jnp.bfloat16
VMEM = pl.BlockSpec(memory_space=pltpu.VMEM)
PARAMS = pltpu.CompilerParams(vmem_limit_bytes=24 * 1024 * 1024)
CONTRACT_LAST = (((1,), (1,)), ((), ()))


def pinned(x):
    return pltpu.with_memory_space_constraint(x, pltpu.VMEM)


def unit(values):
    wide = values.astype(F32)
    return (wide * lax.rsqrt(jnp.sum(wide * wide, axis=1, keepdims=True) + 1e-06)).astype(BF16)


def norm_kernel(teach_ref, stud_ref, proto_ref, teach_out, stud_out, proto_out):
    core = lax.axis_index("core")
    teach = unit(teach_ref[pl.ds(pl.multiple_of(core * TOK_HALF, TOK_HALF), TOK_HALF), :])
    for z in range(NZ):
        teach_out[z] = teach
    stud_out[...] = unit(stud_ref[...])
    proto_out[...] = unit(proto_ref[...])


def to_rows(values):
    return jnp.sum(values.T, axis=0, keepdims=True)


def to_cols(row):
    return jnp.broadcast_to(row, (LANES, LANES)).T


def block_row(step, which):
    core = lax.axis_index("core")
    owner = core if which == 0 else 1 - core
    place = lax.rem(lax.axis_index("y") + (NY - step), NY)
    return pl.multiple_of(owner * HALF + place * PRO_BLOCK, PRO_BLOCK)


def teacher_kernel(teach_ref, *refs):
    protos, (expo_ref, sums_ref) = refs[:NY], refs[NY:]
    teach = teach_ref[...].reshape(TOK, K)
    for step in range(NY):
        for which in range(NC):
            base = block_row(step, which)
            logits = lax.dot_general(
                protos[step][which * PRO_BLOCK : (which + 1) * PRO_BLOCK, :],
                teach,
                CONTRACT_LAST,
                preferred_element_type=F32,
            )
            expo_ref[pl.ds(base, PRO_BLOCK), :] = jnp.exp2(logits * (LOG2E / TEMP_TEACHER))
    col_sums(expo_ref, None, sums_ref)


def col_sums(expo_ref, weights, sums_ref):
    def group(i, carry):
        rows = pl.ds(pl.multiple_of(i * LANES, LANES), LANES)
        total = None
        for j in range(TROWS):
            term = expo_ref[rows, j * LANES : (j + 1) * LANES]
            if weights is not None:
                term = term * weights[j : j + 1, :]
            total = term if total is None else total + term
        sums_ref[0, pl.ds(i, 1), :] = to_rows(total)
        return carry

    lax.fori_loop(0, PROWS, group, 0, unroll=2)
    for peer in range(1, TGROUP):
        sums_ref[peer] = sums_ref[0]


def col_kernel(row_sums_ref, expo_ref, sums_ref):
    weights = 1.0 / jnp.sum(row_sums_ref[...], axis=0)
    col_sums(expo_ref, weights, sums_ref)


def row_sums(expo_ref, weights_ref):
    def group(i, totals):
        rows = pl.ds(pl.multiple_of(i * LANES, LANES), LANES)
        wide = to_cols(weights_ref[pl.ds(i, 1), :])
        out = []
        for j in range(TROWS):
            term = expo_ref[rows, j * LANES : (j + 1) * LANES] * wide
            out.append(totals[j] + jnp.sum(term.reshape(LANES // 8, 8, LANES), axis=0))
        return tuple(out)

    zero = jnp.zeros((8, LANES), F32)
    totals = lax.fori_loop(0, PROWS, group, (zero,) * TROWS, unroll=2)
    return jnp.concatenate([jnp.sum(t, axis=0, keepdims=True) for t in totals], axis=0)


def row_kernel(col_sums_ref, expo_ref, sums_ref, weights_ref):
    weights_ref[...] = 1.0 / jnp.sum(col_sums_ref[...], axis=0)
    sums = row_sums(expo_ref, weights_ref)
    for peer in range(PGROUP):
        sums_ref[peer] = sums


def last_row_kernel(col_sums_ref, expo_ref, stud_sums_ref, sums_ref, weights_ref):
    weights_ref[...] = 1.0 / jnp.sum(col_sums_ref[...], axis=0)
    sums = jnp.concatenate([row_sums(expo_ref, weights_ref), stud_sums_ref[...]], axis=0)
    for peer in range(PGROUP):
        sums_ref[peer] = sums


def student_kernel(stud_ref, *refs):
    protos, (expz_ref, stud_out, sums_ref) = refs[:NY], refs[NY:]
    core = lax.axis_index("core")
    half = pl.ds(pl.multiple_of(core * TOK_HALF, TOK_HALF), TOK_HALF)
    for z in range(NZ):
        stud_out[z * TOK_HALF : (z + 1) * TOK_HALF, :] = stud_ref[z, half, :]
    stud = stud_out[...]
    totals = [jnp.zeros((8, LANES), F32)] * TROWS
    for step in range(NY):
        for which in range(NC):
            base = block_row(step, which)
            logits = lax.dot_general(
                protos[step][which * PRO_BLOCK : (which + 1) * PRO_BLOCK, :],
                stud,
                CONTRACT_LAST,
                preferred_element_type=F32,
            )
            expz = jnp.exp2(logits * (LOG2E / TEMP_STUDENT))
            expz_ref[pl.ds(base, PRO_BLOCK), :] = expz
            for j in range(TROWS):
                part = expz[:, j * LANES : (j + 1) * LANES]
                totals[j] = totals[j] + jnp.sum(part.reshape(PRO_BLOCK // 8, 8, LANES), axis=0)
    sums_ref[...] = jnp.concatenate([jnp.sum(t, axis=0, keepdims=True) for t in totals], axis=0)


def grad_kernel(other, col_sums_ref, row_sums_ref, expo_ref, expz_ref, stud_ref, out_ref, weights_ref):
    core = lax.axis_index("core")
    owner = 1 - core if other else core
    weights_ref[...] = 1.0 / jnp.sum(col_sums_ref[...], axis=0)
    totals = jnp.sum(row_sums_ref[...], axis=0)
    target_scale = SCALE / totals[:TROWS]
    prob_scale = SCALE / totals[TROWS:]
    stud = stud_ref[...]
    block = 256
    for i in range(HALF // block):
        base = pl.multiple_of(owner * HALF + i * block, block)
        parts = []
        for k in range(block // LANES):
            wide = to_cols(weights_ref[pl.ds(owner * (HALF // LANES) + i * (block // LANES) + k, 1), :])
            rows = pl.ds(pl.multiple_of(base + k * LANES, LANES), LANES)
            cols = []
            for j in range(TROWS):
                lanes = slice(j * LANES, (j + 1) * LANES)
                target = (expo_ref[rows, lanes] * wide) * target_scale[j : j + 1, :]
                prob = expz_ref[rows, lanes] * prob_scale[j : j + 1, :]
                cols.append((prob - target).astype(BF16))
            parts.append(jnp.concatenate(cols, axis=1))
        grads = jnp.concatenate(parts, axis=0)
        out_ref[i * block : (i + 1) * block, :] = jnp.dot(grads, stud, preferred_element_type=F32)


def call(kernel, out_shape, *args, scratch=()):
    return pl.pallas_call(
        kernel,
        out_shape=out_shape,
        in_specs=[VMEM] * len(args),
        out_specs=jax.tree.map(lambda _: VMEM, out_shape),
        scratch_shapes=scratch,
        compiler_params=PARAMS,
    )(*args)


def shards(teacher_feats, student_feats, prototypes):
    struct = jax.ShapeDtypeStruct
    teach, stud, own = call(
        norm_kernel,
        (
            struct((NZ, TOK_HALF, K), BF16),
            struct((TOK_BLOCK, K), BF16),
            struct((PRO_BLOCK, K), BF16),
        ),
        teacher_feats,
        student_feats,
        prototypes,
    )
    other = lax.ppermute(own, "core", [(0, 1), (1, 0)])
    pair = jnp.concatenate([own, other], axis=0)
    protos = [pair] + [
        lax.ppermute(pair, "y", [(i, (i + step) % NY) for i in range(NY)]) for step in range(1, NY)
    ]
    teach = lax.all_to_all(teach, "z", 0, 0, tiled=True)
    teach, stud = lax.optimization_barrier((teach, stud))
    stud_all = lax.all_gather(stud, "z", axis=0)

    col_shape = struct((TGROUP, PROWS, LANES), F32)
    row_shape = struct((PGROUP, TROWS, LANES), F32)
    weights = pltpu.VMEM((PROWS, LANES), F32)

    expo, cols = call(
        teacher_kernel, (pltpu.VMEM((PRO, TOK), F32), col_shape), teach, *protos
    )
    cols = lax.all_to_all(cols, ("y", "core"), 0, 0, tiled=True)
    for _ in range(ITERS - 1):
        rows = call(row_kernel, row_shape, cols, pinned(expo), scratch=(weights,))
        rows = lax.all_to_all(rows, ("z", "x"), 0, 0, tiled=True)
        cols = call(col_kernel, col_shape, rows, pinned(expo))
        cols = lax.all_to_all(cols, ("y", "core"), 0, 0, tiled=True)
    expz, stud_rows, stud_sums = call(
        student_kernel,
        (pltpu.VMEM((PRO, TOK), F32), struct((TOK, K), BF16), struct((TROWS, LANES), F32)),
        stud_all,
        *protos,
    )
    rows = call(
        last_row_kernel,
        struct((PGROUP, 2 * TROWS, LANES), F32),
        cols,
        pinned(expo),
        stud_sums,
        scratch=(weights,),
    )
    rows = lax.all_to_all(rows, ("z", "x"), 0, 0, tiled=True)

    def grad(for_other):
        return call(
            functools.partial(grad_kernel, for_other),
            struct((HALF, K), F32),
            cols,
            rows,
            pinned(expo),
            pinned(expz),
            stud_rows,
            scratch=(weights,),
        )

    sent = lax.ppermute(grad(True), "core", [(0, 1), (1, 0)])
    total = (grad(False) + sent).reshape(NY, PRO_BLOCK, K)
    parts = lax.all_to_all(total.astype(BF16), "y", 0, 0, tiled=True)
    return jnp.sum(parts.astype(F32), axis=0)


def solution(mesh):
    grid = Mesh(mesh.devices.reshape(NZ, NY, NX, NC), ("z", "y", "x", "core"))
    tokens = P(("z", "y"), None)
    protos = P(("z", "y", "x", "core"), None)
    return jax.shard_map(
        shards, mesh=grid, in_specs=(tokens, tokens, protos), out_specs=protos, check_vma=False
    )
```

```python
import functools
import math

import jax
import jax.numpy as jnp
from jax import lax
from jax.experimental import pallas as pl
from jax.experimental.pallas import tpu as pltpu
from jax.sharding import Mesh, PartitionSpec as P

K = 384
PROTO = 65536
TOKENS = 8192
ITERS = 3
TEMP_TEACHER = 0.07
TEMP_STUDENT = 0.1
LOG2E = math.log2(math.e)
SCALE = PROTO / (TEMP_STUDENT * math.sqrt(TOKENS))

NZ, NY, NX, NC = 8, 4, 4, 2
TOK_BLOCK = TOKENS // (NZ * NY)
TOK_HALF = TOK_BLOCK // NC
PRO_BLOCK = PROTO // (NZ * NY * NX * NC)
TOK = TOK_HALF * NZ
PRO = PRO_BLOCK * NY * NC
HALF = PRO // 2
LANES = 128
TROWS = TOK // LANES
PROWS = PRO // LANES
TGROUP = NY * NC
PGROUP = NZ * NX

F32 = jnp.float32
BF16 = jnp.bfloat16
VMEM = pl.BlockSpec(memory_space=pltpu.VMEM)
PARAMS = pltpu.CompilerParams(vmem_limit_bytes=24 * 1024 * 1024)
CONTRACT_LAST = (((1,), (1,)), ((), ()))


def pinned(x):
    return pltpu.with_memory_space_constraint(x, pltpu.VMEM)


def unit(values):
    wide = values.astype(F32)
    return (wide * lax.rsqrt(jnp.sum(wide * wide, axis=1, keepdims=True) + 1e-06)).astype(BF16)


def norm_kernel(teach_hbm, stud_hbm, teach_out, stud_out, teach_buf, stud_buf, sems):
    half = pl.ds(pl.multiple_of(lax.axis_index("core") * TOK_HALF, TOK_HALF), TOK_HALF)
    first = pltpu.make_async_copy(teach_hbm.at[half, :], teach_buf, sems.at[0])
    second = pltpu.make_async_copy(stud_hbm.at[half, :], stud_buf, sems.at[1])
    first.start()
    second.start()
    first.wait()
    teach = unit(teach_buf[...])
    for z in range(NZ):
        teach_out[z] = teach
    second.wait()
    stud_out[...] = unit(stud_buf[...])


def to_rows(values):
    return jnp.sum(values.T, axis=0, keepdims=True)


def to_cols(row):
    return jnp.broadcast_to(row, (LANES, LANES)).T


def block_row(step, which):
    core = lax.axis_index("core")
    owner = core if which == 0 else 1 - core
    place = lax.rem(lax.axis_index("y") + (NY - step), NY)
    return pl.multiple_of(owner * HALF + place * PRO_BLOCK, PRO_BLOCK)


def teacher_kernel(teach_ref, *refs):
    raw, (expo_ref, unit_ref, sums_ref, protos, sems) = refs[:NY], refs[NY:]
    copies = [pltpu.make_async_copy(raw[i], protos.at[i], sems.at[i]) for i in range(NY)]
    for copy in copies:
        copy.start()
    teach = teach_ref[...].reshape(TOK, K)
    for step in range(NY):
        copies[step].wait()
        for which in range(NC):
            base = block_row(step, which)
            proto = unit(protos[step, which * PRO_BLOCK : (which + 1) * PRO_BLOCK, :])
            unit_ref[pl.ds(base, PRO_BLOCK), :] = proto
            logits = lax.dot_general(
                proto,
                teach,
                CONTRACT_LAST,
                preferred_element_type=F32,
            )
            expo_ref[pl.ds(base, PRO_BLOCK), :] = jnp.exp2(logits * (LOG2E / TEMP_TEACHER))
    col_sums(expo_ref, None, sums_ref)


def col_sums(expo_ref, weights, sums_ref):
    def group(i, carry):
        rows = pl.ds(pl.multiple_of(i * LANES, LANES), LANES)
        total = None
        for j in range(TROWS):
            term = expo_ref[rows, j * LANES : (j + 1) * LANES]
            if weights is not None:
                term = term * weights[j : j + 1, :]
            total = term if total is None else total + term
        sums_ref[0, pl.ds(i, 1), :] = to_rows(total)
        return carry

    lax.fori_loop(0, PROWS, group, 0, unroll=2)
    for peer in range(1, TGROUP):
        sums_ref[peer] = sums_ref[0]


def col_kernel(row_sums_ref, expo_ref, sums_ref):
    weights = 1.0 / jnp.sum(row_sums_ref[...].astype(F32), axis=0)
    col_sums(expo_ref, weights, sums_ref)


def row_sums(expo_ref, weights_ref):
    def group(i, totals):
        rows = pl.ds(pl.multiple_of(i * LANES, LANES), LANES)
        wide = to_cols(weights_ref[pl.ds(i, 1), :])
        out = []
        for j in range(TROWS):
            term = expo_ref[rows, j * LANES : (j + 1) * LANES] * wide
            out.append(totals[j] + jnp.sum(term.reshape(LANES // 8, 8, LANES), axis=0))
        return tuple(out)

    zero = jnp.zeros((8, LANES), F32)
    totals = lax.fori_loop(0, PROWS, group, (zero,) * TROWS, unroll=2)
    return jnp.concatenate([jnp.sum(t, axis=0, keepdims=True) for t in totals], axis=0)


def row_kernel(col_sums_ref, expo_ref, sums_ref, weights_ref):
    weights_ref[...] = 1.0 / jnp.sum(col_sums_ref[...], axis=0)
    sums = row_sums(expo_ref, weights_ref).astype(BF16)
    for peer in range(PGROUP):
        sums_ref[peer] = sums


def last_row_kernel(*refs):
    pieces, (col_sums_ref, proto_ref, expo_ref), outs = refs[:4], refs[4:7], refs[7:]
    expz_ref, stud_out, sums_ref, weights_ref = outs
    place = lax.axis_index("z")
    offsets = [0]
    for piece, hop in zip(pieces, (0, 4, 2, 1)):
        hops = [o ^ hop for o in offsets]
        for i, hop_to in enumerate(hops):
            rows = pl.ds(pl.multiple_of((place ^ hop_to) * TOK_HALF, TOK_HALF), TOK_HALF)
            stud_out[rows, :] = piece[i * TOK_HALF : (i + 1) * TOK_HALF, :]
        if hop:
            offsets = offsets + hops
    stud = stud_out[...]
    weights_ref[...] = 1.0 / jnp.sum(col_sums_ref[...], axis=0)
    totals = [jnp.zeros((8, LANES), F32)] * TROWS
    for i in range(PRO // PRO_BLOCK):
        rows = slice(i * PRO_BLOCK, (i + 1) * PRO_BLOCK)
        logits = lax.dot_general(
            proto_ref[rows, :], stud, CONTRACT_LAST, preferred_element_type=F32
        )
        expz = jnp.exp2(logits * (LOG2E / TEMP_STUDENT))
        expz_ref[rows, :] = expz
        for j in range(TROWS):
            part = expz[:, j * LANES : (j + 1) * LANES]
            totals[j] = totals[j] + jnp.sum(part.reshape(PRO_BLOCK // 8, 8, LANES), axis=0)
    stud_sums = [jnp.sum(t, axis=0, keepdims=True) for t in totals]
    sums = jnp.concatenate([row_sums(expo_ref, weights_ref)] + stud_sums, axis=0).astype(BF16)
    for peer in range(PGROUP):
        sums_ref[peer] = sums


def grad_kernel(other, col_sums_ref, row_sums_ref, expo_ref, expz_ref, stud_ref, *refs):
    outs, weights_ref = refs[:NY], refs[NY]
    core = lax.axis_index("core")
    owner = 1 - core if other else core
    weights_ref[...] = 1.0 / jnp.sum(col_sums_ref[...], axis=0)
    totals = jnp.sum(row_sums_ref[...].astype(F32), axis=0)
    target_scale = SCALE / totals[:TROWS]
    prob_scale = SCALE / totals[TROWS:]
    stud = stud_ref[...]
    for step in range(NY):
        place = lax.rem(lax.axis_index("y") + step, NY)
        group = owner * (HALF // LANES) + place * (PRO_BLOCK // LANES)
        parts = []
        for k in range(PRO_BLOCK // LANES):
            wide = to_cols(weights_ref[pl.ds(group + k, 1), :])
            rows = pl.ds(pl.multiple_of((group + k) * LANES, LANES), LANES)
            cols = []
            for j in range(TROWS):
                lanes = slice(j * LANES, (j + 1) * LANES)
                target = (expo_ref[rows, lanes] * wide) * target_scale[j : j + 1, :]
                prob = expz_ref[rows, lanes] * prob_scale[j : j + 1, :]
                cols.append((prob - target).astype(BF16))
            parts.append(jnp.concatenate(cols, axis=1))
        grads = jnp.concatenate(parts, axis=0)
        outs[step][...] = jnp.dot(grads, stud, preferred_element_type=F32)


def call(kernel, out_shape, *args, scratch=(), specs=None):
    return pl.pallas_call(
        kernel,
        out_shape=out_shape,
        in_specs=specs or [VMEM] * len(args),
        out_specs=jax.tree.map(lambda _: VMEM, out_shape),
        scratch_shapes=scratch,
        compiler_params=PARAMS,
    )(*args)


def shift(x, axis, size, step):
    return lax.ppermute(x, axis, [(i, (i + step) % size) for i in range(size)])


def shards(teacher_feats, student_feats, prototypes):
    struct = jax.ShapeDtypeStruct
    other = shift(prototypes, "core", NC, 1)
    half = pltpu.VMEM((TOK_HALF, K), BF16)
    teach, stud = call(
        norm_kernel,
        (struct((NZ, TOK_HALF, K), BF16), struct((TOK_HALF, K), BF16)),
        pltpu.with_memory_space_constraint(teacher_feats, pltpu.HBM),
        pltpu.with_memory_space_constraint(student_feats, pltpu.HBM),
        scratch=(half, half, pltpu.SemaphoreType.DMA((2,))),
        specs=[pl.BlockSpec(memory_space=pl.ANY)] * 2,
    )
    pair = jnp.concatenate([prototypes, other], axis=0)
    pair, teach = lax.optimization_barrier((pair, teach))
    protos = [pair] + [shift(pair, "y", NY, step) for step in range(1, NY)]
    teach = lax.all_to_all(teach, "z", 0, 0, tiled=True)
    teach, stud = lax.optimization_barrier((teach, stud))

    col_shape = struct((TGROUP, PROWS, LANES), F32)
    row_shape = struct((PGROUP, TROWS, LANES), BF16)
    weights = pltpu.VMEM((PROWS, LANES), F32)

    expo, protos, cols = call(
        teacher_kernel,
        (pltpu.VMEM((PRO, TOK), F32), struct((PRO, K), BF16), col_shape),
        teach,
        *[pltpu.with_memory_space_constraint(p, pltpu.HBM) for p in protos],
        scratch=(pltpu.VMEM((NY, NC * PRO_BLOCK, K), BF16), pltpu.SemaphoreType.DMA((NY,))),
        specs=[VMEM] + [pl.BlockSpec(memory_space=pl.ANY)] * NY,
    )
    pieces = [stud]
    held = stud
    for step, hop in enumerate((4, 2, 1)):
        cols, held = lax.optimization_barrier((cols, held))
        got = lax.ppermute(held, "z", [(i, i ^ hop) for i in range(NZ)])
        cols = lax.all_to_all(cols, ("y", "core"), 0, 0, tiled=True)
        cols, got = lax.optimization_barrier((cols, got))
        pieces.append(got)
        if step + 1 < ITERS:
            rows = call(row_kernel, row_shape, cols, pinned(expo), scratch=(weights,))
            held = jnp.concatenate(pieces, axis=0)
            rows, held = lax.optimization_barrier((rows, held))
            rows = lax.all_to_all(rows, ("z", "x"), 0, 0, tiled=True)
            cols = call(col_kernel, col_shape, rows, pinned(expo))
    expz, stud, rows = call(
        last_row_kernel,
        (
            pltpu.VMEM((PRO, TOK), F32),
            struct((TOK, K), BF16),
            struct((PGROUP, 2 * TROWS, LANES), BF16),
        ),
        *pieces,
        cols,
        protos,
        pinned(expo),
        scratch=(weights,),
    )
    rows = lax.all_to_all(rows, ("z", "x"), 0, 0, tiled=True)

    def grad(for_other):
        return call(
            functools.partial(grad_kernel, for_other),
            (struct((PRO_BLOCK, K), F32),) * NY,
            cols,
            rows,
            pinned(expo),
            pinned(expz),
            stud,
            scratch=(weights,),
        )

    sent = [shift(part, "core", NC, 1) for part in grad(True)]
    parts = [mine + part for mine, part in zip(grad(False), sent)]
    total = parts[0]
    for step in (2, 1, 3):
        total = total + shift(parts[step].astype(BF16), "y", NY, step).astype(F32)
    return total


def solution(mesh):
    grid = Mesh(mesh.devices.reshape(NZ, NY, NX, NC), ("z", "y", "x", "core"))
    tokens = P(("z", "y"), None)
    protos = P(("z", "y", "x", "core"), None)
    return jax.shard_map(
        shards, mesh=grid, in_specs=(tokens, tokens, protos), out_specs=protos, check_vma=False
    )
```

```python
import functools
import math

import jax
import jax.numpy as jnp
from jax import lax
from jax.experimental import pallas as pl
from jax.experimental.pallas import tpu as pltpu
from jax.sharding import Mesh, PartitionSpec as P

K = 384
PROTO = 65536
TOKENS = 8192
ITERS = 3
TEMP_TEACHER = 0.07
TEMP_STUDENT = 0.1
LOG2E = math.log2(math.e)
SCALE = PROTO / (TEMP_STUDENT * math.sqrt(TOKENS))

NZ, NY, NX, NC = 8, 4, 4, 2
TOK_BLOCK = TOKENS // (NZ * NY)
TOK_HALF = TOK_BLOCK // NC
PRO_BLOCK = PROTO // (NZ * NY * NX * NC)
TOK = TOK_HALF * NZ
PRO = PRO_BLOCK * NY * NC
HALF = PRO // 2
LANES = 128
TROWS = TOK // LANES
PROWS = PRO // LANES
HROWS = HALF // LANES
TGROUP = NY * NC
PGROUP = NZ * NX

F32 = jnp.float32
BF16 = jnp.bfloat16
VMEM = pl.BlockSpec(memory_space=pltpu.VMEM)
PARAMS = pltpu.CompilerParams(vmem_limit_bytes=24 * 1024 * 1024)
CONTRACT_LAST = (((1,), (1,)), ((), ()))


def pinned(x):
    return pltpu.with_memory_space_constraint(x, pltpu.VMEM)


def unit(values):
    wide = values.astype(F32)
    return (wide * lax.rsqrt(jnp.sum(wide * wide, axis=1, keepdims=True) + 1e-06)).astype(BF16)


def norm_kernel(teach_hbm, stud_hbm, proto_hbm, teach_out, stud_out, proto_out, teach_buf, stud_buf, sems):
    half = pl.ds(pl.multiple_of(lax.axis_index("core") * TOK_HALF, TOK_HALF), TOK_HALF)
    copies = [
        pltpu.make_async_copy(teach_hbm.at[half, :], teach_buf, sems.at[0]),
        pltpu.make_async_copy(stud_hbm.at[half, :], stud_buf, sems.at[1]),
        pltpu.make_async_copy(proto_hbm, proto_out, sems.at[2]),
    ]
    for copy in copies:
        copy.start()
    copies[0].wait()
    teach = unit(teach_buf[...])
    for z in range(NZ):
        teach_out[z] = teach
    copies[1].wait()
    stud_out[...] = unit(stud_buf[...])
    copies[2].wait()


def to_rows(values):
    return jnp.sum(values.T, axis=0, keepdims=True)


def to_cols(row):
    return jnp.broadcast_to(row, (LANES, LANES)).T


def own_first(core, which):
    return core if which == 0 else 1 - core


def block_row(step):
    place = lax.rem(lax.axis_index("y") + (NY - step), NY)
    return pl.multiple_of(place * PRO_BLOCK, PRO_BLOCK)


def teacher_kernel(teach_ref, *refs):
    raw, (expo_ref, unit_ref, sums_ref) = refs[:NY], refs[NY:]
    teach = teach_ref[...].reshape(TOK, K)
    for step in range(NY):
        base = block_row(step)
        rows = pl.ds(base, PRO_BLOCK)
        proto = unit(raw[step][...])
        unit_ref[rows, :] = proto
        logits = lax.dot_general(proto, teach, CONTRACT_LAST, preferred_element_type=F32)
        expo = jnp.exp2(logits * (LOG2E / TEMP_TEACHER))
        expo_ref[rows, :] = expo
        total = sum(expo[:, j * LANES : (j + 1) * LANES] for j in range(TROWS))
        for k in range(PRO_BLOCK // LANES):
            sums_ref[pl.ds(base // LANES + k, 1), :] = to_rows(total[k * LANES : (k + 1) * LANES, :])


def second_teacher_kernel(teach_ref, *refs):
    raw, first_ref, (expo_ref, unit_ref, sums_ref, second_ref) = refs[:NY], refs[NY], refs[NY + 1 :]
    teacher_kernel(teach_ref, *raw, expo_ref, unit_ref, second_ref)
    core = lax.axis_index("core")
    for peer in range(TGROUP):
        for which, part_ref in enumerate((first_ref, second_ref)):
            base = pl.multiple_of(own_first(core, which) * HROWS, HROWS)
            sums_ref[peer, pl.ds(base, HROWS), :] = part_ref[...]


def col_sums(expo_refs, weights, sums_ref):
    core = lax.axis_index("core")
    for which, expo_ref in enumerate(expo_refs):
        base = own_first(core, which) * HROWS

        def group(i, carry):
            rows = pl.ds(pl.multiple_of(i * LANES, LANES), LANES)
            total = None
            for j in range(TROWS):
                term = expo_ref[rows, j * LANES : (j + 1) * LANES] * weights[j : j + 1, :]
                total = term if total is None else total + term
            sums_ref[0, pl.ds(base + i, 1), :] = to_rows(total)
            return carry

        lax.fori_loop(0, HROWS, group, 0, unroll=True)
    for peer in range(1, TGROUP):
        sums_ref[peer] = sums_ref[0]


def col_kernel(row_sums_ref, first_ref, second_ref, sums_ref):
    weights = 1.0 / jnp.sum(row_sums_ref[...].astype(F32), axis=0)
    col_sums((first_ref, second_ref), weights, sums_ref)


def row_sums(expo_refs, weights_ref):
    core = lax.axis_index("core")
    totals = (jnp.zeros((8, LANES), F32),) * TROWS
    for which, expo_ref in enumerate(expo_refs):
        base = own_first(core, which) * HROWS

        def group(i, totals):
            rows = pl.ds(pl.multiple_of(i * LANES, LANES), LANES)
            wide = to_cols(weights_ref[pl.ds(base + i, 1), :])
            out = []
            for j in range(TROWS):
                term = expo_ref[rows, j * LANES : (j + 1) * LANES] * wide
                out.append(totals[j] + jnp.sum(term.reshape(LANES // 8, 8, LANES), axis=0))
            return tuple(out)

        totals = lax.fori_loop(0, HROWS, group, totals, unroll=True)
    return jnp.concatenate([jnp.sum(t, axis=0, keepdims=True) for t in totals], axis=0)


def row_kernel(col_sums_ref, first_ref, second_ref, sums_ref, weights_ref):
    weights_ref[...] = 1.0 / jnp.sum(col_sums_ref[...], axis=0)
    sums = row_sums((first_ref, second_ref), weights_ref).astype(BF16)
    for peer in range(PGROUP):
        sums_ref[peer] = sums


def last_row_kernel(*refs):
    pieces, (col_sums_ref, *protos), expos, outs = refs[:4], refs[4:7], refs[7:9], refs[9:]
    *expzs, stud_out, sums_ref, weights_ref = outs
    place = lax.axis_index("z")
    offsets = [0]
    for piece, hop in zip(pieces, (0, 4, 2, 1)):
        hops = [o ^ hop for o in offsets]
        for i, hop_to in enumerate(hops):
            rows = pl.ds(pl.multiple_of((place ^ hop_to) * TOK_HALF, TOK_HALF), TOK_HALF)
            stud_out[rows, :] = piece[i * TOK_HALF : (i + 1) * TOK_HALF, :]
        if hop:
            offsets = offsets + hops
    stud = stud_out[...]
    weights_ref[...] = 1.0 / jnp.sum(col_sums_ref[...], axis=0)
    totals = [jnp.zeros((8, LANES), F32)] * TROWS
    for i in range(PRO // PRO_BLOCK):
        proto_ref, expz_ref = protos[i // NY], expzs[i // NY]
        rows = slice(i % NY * PRO_BLOCK, (i % NY + 1) * PRO_BLOCK)
        logits = lax.dot_general(
            proto_ref[rows, :], stud, CONTRACT_LAST, preferred_element_type=F32
        )
        expz = jnp.exp2(logits * (LOG2E / TEMP_STUDENT))
        expz_ref[rows, :] = expz
        for j in range(TROWS):
            part = expz[:, j * LANES : (j + 1) * LANES]
            totals[j] = totals[j] + jnp.sum(part.reshape(PRO_BLOCK // 8, 8, LANES), axis=0)
    stud_sums = [jnp.sum(t, axis=0, keepdims=True) for t in totals]
    sums = jnp.concatenate([row_sums(expos, weights_ref)] + stud_sums, axis=0).astype(BF16)
    for peer in range(PGROUP):
        sums_ref[peer] = sums


def grad_kernel(tasks, col_sums_ref, row_sums_ref, stud_ref, *refs):
    expos, expzs, outs, weights_ref = refs[:2], refs[2:4], refs[4:-1], refs[-1]
    core = lax.axis_index("core")
    weights_ref[...] = 1.0 / jnp.sum(col_sums_ref[...], axis=0)
    totals = jnp.sum(row_sums_ref[...].astype(F32), axis=0)
    target_scale = SCALE / totals[:TROWS]
    prob_scale = SCALE / totals[TROWS:]
    stud = stud_ref[...]
    for (which, step), out_ref in zip(tasks, outs):
        expo_ref, expz_ref = expos[which], expzs[which]
        base = own_first(core, which) * HROWS
        group = lax.rem(lax.axis_index("y") + step, NY) * (PRO_BLOCK // LANES)
        parts = []
        for k in range(PRO_BLOCK // LANES):
            wide = to_cols(weights_ref[pl.ds(base + group + k, 1), :])
            rows = pl.ds(pl.multiple_of((group + k) * LANES, LANES), LANES)
            cols = []
            for j in range(TROWS):
                lanes = slice(j * LANES, (j + 1) * LANES)
                target = (expo_ref[rows, lanes] * wide) * target_scale[j : j + 1, :]
                prob = expz_ref[rows, lanes] * prob_scale[j : j + 1, :]
                cols.append((prob - target).astype(BF16))
            parts.append(jnp.concatenate(cols, axis=1))
        grads = jnp.concatenate(parts, axis=0)
        out_ref[...] = jnp.dot(grads, stud, preferred_element_type=F32)


def call(kernel, out_shape, *args, scratch=(), specs=None):
    return pl.pallas_call(
        kernel,
        out_shape=out_shape,
        in_specs=specs or [VMEM] * len(args),
        out_specs=jax.tree.map(lambda _: VMEM, out_shape),
        scratch_shapes=scratch,
        compiler_params=PARAMS,
    )(*args)


def shift(x, axis, size, step):
    return lax.ppermute(x, axis, [(i, (i + step) % size) for i in range(size)])


def shards(teacher_feats, student_feats, prototypes):
    struct = jax.ShapeDtypeStruct
    near = [prototypes] + [shift(prototypes, "y", NY, step) for step in range(1, NY)]
    half = pltpu.VMEM((TOK_HALF, K), BF16)
    teach, stud, near[0] = call(
        norm_kernel,
        (
            struct((NZ, TOK_HALF, K), BF16),
            struct((TOK_HALF, K), BF16),
            struct((PRO_BLOCK, K), BF16),
        ),
        *[
            pltpu.with_memory_space_constraint(x, pltpu.HBM)
            for x in (teacher_feats, student_feats, prototypes)
        ],
        scratch=(half, half, pltpu.SemaphoreType.DMA((3,))),
        specs=[pl.BlockSpec(memory_space=pl.ANY)] * 3,
    )
    teach = lax.all_to_all(teach, "z", 0, 0, tiled=True)
    teach, stud = lax.optimization_barrier((teach, stud))
    far = [shift(proto, "core", NC, 1) for proto in near]

    col_shape = struct((TGROUP, PROWS, LANES), F32)
    row_shape = struct((PGROUP, TROWS, LANES), BF16)
    weights = pltpu.VMEM((PROWS, LANES), F32)

    square = pltpu.VMEM((HALF, TOK), F32)
    unit_shape = struct((HALF, K), BF16)
    half_sums = struct((HROWS, LANES), F32)
    near_expo, near, near_sums = call(
        teacher_kernel, (square, unit_shape, half_sums), teach, *near
    )
    far_expo, far, cols = call(
        second_teacher_kernel,
        (square, unit_shape, col_shape),
        teach,
        *far,
        near_sums,
        scratch=(pltpu.VMEM((HROWS, LANES), F32),),
    )
    pieces = [stud]
    held = stud
    for step, hop in enumerate((4, 2, 1)):
        if step:
            cols, held = lax.optimization_barrier((cols, held))
        got = lax.ppermute(held, "z", [(i, i ^ hop) for i in range(NZ)])
        cols = lax.all_to_all(cols, ("y", "core"), 0, 0, tiled=True)
        cols, got = lax.optimization_barrier((cols, got))
        pieces.append(got)
        if step + 1 < ITERS:
            rows = call(
                row_kernel, row_shape, cols, pinned(near_expo), pinned(far_expo), scratch=(weights,)
            )
            held = jnp.concatenate(pieces, axis=0)
            rows, held = lax.optimization_barrier((rows, held))
            rows = lax.all_to_all(rows, ("z", "x"), 0, 0, tiled=True)
            cols = call(col_kernel, col_shape, rows, pinned(near_expo), pinned(far_expo))
    near_expz, far_expz, stud, rows = call(
        last_row_kernel,
        (
            square,
            square,
            struct((TOK, K), BF16),
            struct((PGROUP, 2 * TROWS, LANES), BF16),
        ),
        *pieces,
        cols,
        near,
        far,
        pinned(near_expo),
        pinned(far_expo),
        scratch=(weights,),
    )
    rows = lax.all_to_all(rows, ("z", "x"), 0, 0, tiled=True)

    def grad(*tasks):
        return call(
            functools.partial(grad_kernel, tasks),
            (struct((PRO_BLOCK, K), F32),) * len(tasks),
            cols,
            rows,
            stud,
            *[pinned(x) for x in (near_expo, far_expo, near_expz, far_expz)],
            scratch=(weights,),
        )

    far = [shift(part, "core", NC, 1) for part in grad((1, 2), (1, 1), (1, 3), (1, 0))]
    parts = [near + part for near, part in zip(grad((0, 2), (0, 1), (0, 3), (0, 0)), far)]
    total = parts[3]
    for part, step in zip(parts, (2, 1, 3)):
        total = total + shift(part.astype(BF16), "y", NY, step).astype(F32)
    return total


def solution(mesh):
    grid = Mesh(mesh.devices.reshape(NZ, NY, NX, NC), ("z", "y", "x", "core"))
    tokens = P(("z", "y"), None)
    protos = P(("z", "y", "x", "core"), None)
    return jax.shard_map(
        shards, mesh=grid, in_specs=(tokens, tokens, protos), out_specs=protos, check_vma=False
    )
```

```python
import functools
import math

import jax
import jax.numpy as jnp
from jax import lax
from jax.experimental import pallas as pl
from jax.experimental.pallas import tpu as pltpu
from jax.sharding import Mesh, PartitionSpec as P

K = 384
PROTO = 65536
TOKENS = 8192
ITERS = 3
TEMP_TEACHER = 0.07
TEMP_STUDENT = 0.1
LOG2E = math.log2(math.e)
SCALE = PROTO / (TEMP_STUDENT * math.sqrt(TOKENS))

NZ, NY, NX, NC = 8, 4, 4, 2
TOK_BLOCK = TOKENS // (NZ * NY)
TOK_HALF = TOK_BLOCK // NC
PRO_BLOCK = PROTO // (NZ * NY * NX * NC)
TOK = TOK_HALF * NZ
PRO = PRO_BLOCK * NY * NC
HALF = PRO // 2
LANES = 128
TROWS = TOK // LANES
PROWS = PRO // LANES
HROWS = HALF // LANES
TGROUP = NY * NC
PGROUP = NZ * NX

F32 = jnp.float32
BF16 = jnp.bfloat16
VMEM = pl.BlockSpec(memory_space=pltpu.VMEM)
ANY = pl.BlockSpec(memory_space=pl.ANY)
PARAMS = pltpu.CompilerParams(vmem_limit_bytes=24 * 1024 * 1024)
CONTRACT_LAST = (((1,), (1,)), ((), ()))


def pinned(x):
    return pltpu.with_memory_space_constraint(x, pltpu.VMEM)


def unit(values):
    wide = values.astype(F32)
    return (wide * lax.rsqrt(jnp.sum(wide * wide, axis=1, keepdims=True) + 1e-06)).astype(BF16)


def norm_kernel(teach_hbm, stud_hbm, proto_hbm, teach_out, stud_out, proto_out, teach_buf, stud_buf, sems):
    half = pl.ds(pl.multiple_of(lax.axis_index("core") * TOK_HALF, TOK_HALF), TOK_HALF)
    copies = [
        pltpu.make_async_copy(teach_hbm.at[half, :], teach_buf, sems.at[0]),
        pltpu.make_async_copy(stud_hbm.at[half, :], stud_buf, sems.at[1]),
        pltpu.make_async_copy(proto_hbm, proto_out, sems.at[2]),
    ]
    for copy in copies:
        copy.start()
    copies[0].wait()
    teach_buf[...] = unit(teach_buf[...])
    spread = [pltpu.make_async_copy(teach_buf, teach_out.at[z], sems.at[3 + z]) for z in range(NZ)]
    for copy in spread:
        copy.start()
    copies[1].wait()
    stud_out[...] = unit(stud_buf[...])
    copies[2].wait()
    for copy in spread:
        copy.wait()


def to_rows(values):
    return jnp.sum(values.T, axis=0, keepdims=True)


def to_cols(row):
    return jnp.broadcast_to(row, (LANES, LANES)).T


def own_first(core, which):
    return core if which == 0 else 1 - core


def block_row(step):
    place = lax.rem(lax.axis_index("y") + (NY - step), NY)
    return pl.multiple_of(place * PRO_BLOCK, PRO_BLOCK)


def teacher_kernel(teach_ref, *refs):
    raw, (expo_ref, unit_ref, sums_ref) = refs[:NY], refs[NY:]
    teach = teach_ref[...].reshape(TOK, K)
    for step in range(NY):
        base = block_row(step)
        rows = pl.ds(base, PRO_BLOCK)
        proto = unit(raw[step][...])
        unit_ref[rows, :] = proto
        logits = lax.dot_general(proto, teach, CONTRACT_LAST, preferred_element_type=F32)
        expo = jnp.exp2(logits * (LOG2E / TEMP_TEACHER))
        expo_ref[rows, :] = expo
        total = sum(expo[:, j * LANES : (j + 1) * LANES] for j in range(TROWS))
        for k in range(PRO_BLOCK // LANES):
            sums_ref[pl.ds(base // LANES + k, 1), :] = to_rows(total[k * LANES : (k + 1) * LANES, :])


def second_teacher_kernel(teach_ref, *refs):
    raw, first_ref, (expo_ref, unit_ref, sums_ref, second_ref) = refs[:NY], refs[NY], refs[NY + 1 :]
    teacher_kernel(teach_ref, *raw, expo_ref, unit_ref, second_ref)
    core = lax.axis_index("core")
    for peer in range(TGROUP):
        for which, part_ref in enumerate((first_ref, second_ref)):
            base = pl.multiple_of(own_first(core, which) * HROWS, HROWS)
            sums_ref[peer, pl.ds(base, HROWS), :] = part_ref[...]


def col_sums(expo_refs, weights, sums_ref):
    core = lax.axis_index("core")
    for which, expo_ref in enumerate(expo_refs):
        base = own_first(core, which) * HROWS

        def group(i, carry):
            rows = pl.ds(pl.multiple_of(i * LANES, LANES), LANES)
            total = None
            for j in range(TROWS):
                term = expo_ref[rows, j * LANES : (j + 1) * LANES] * weights[j : j + 1, :]
                total = term if total is None else total + term
            sums_ref[0, pl.ds(base + i, 1), :] = to_rows(total)
            return carry

        lax.fori_loop(0, HROWS, group, 0, unroll=True)
    for peer in range(1, TGROUP):
        sums_ref[peer] = sums_ref[0]


def col_kernel(row_sums_ref, first_ref, second_ref, sums_ref):
    weights = 1.0 / jnp.sum(row_sums_ref[...].astype(F32), axis=0)
    col_sums((first_ref, second_ref), weights, sums_ref)


def row_sums(expo_refs, weights_ref):
    core = lax.axis_index("core")
    totals = (jnp.zeros((8, LANES), F32),) * TROWS
    for which, expo_ref in enumerate(expo_refs):
        base = own_first(core, which) * HROWS

        def group(i, totals):
            rows = pl.ds(pl.multiple_of(i * LANES, LANES), LANES)
            wide = to_cols(weights_ref[pl.ds(base + i, 1), :])
            out = []
            for j in range(TROWS):
                term = expo_ref[rows, j * LANES : (j + 1) * LANES] * wide
                out.append(totals[j] + jnp.sum(term.reshape(LANES // 8, 8, LANES), axis=0))
            return tuple(out)

        totals = lax.fori_loop(0, HROWS, group, totals, unroll=True)
    return jnp.concatenate([jnp.sum(t, axis=0, keepdims=True) for t in totals], axis=0)


def row_kernel(col_sums_ref, first_ref, second_ref, sums_ref, weights_ref):
    weights_ref[...] = 1.0 / jnp.sum(col_sums_ref[...], axis=0)
    sums = row_sums((first_ref, second_ref), weights_ref).astype(BF16)
    for peer in range(PGROUP):
        sums_ref[peer] = sums


def last_row_kernel(*refs):
    pieces, (col_sums_ref, *protos), expos, outs = refs[:4], refs[4:7], refs[7:9], refs[9:]
    *expzs, stud_out, sums_ref, weights_ref = outs
    place = lax.axis_index("z")
    offsets = [0]
    for piece, hop in zip(pieces, (0, 4, 2, 1)):
        hops = [o ^ hop for o in offsets]
        for i, hop_to in enumerate(hops):
            rows = pl.ds(pl.multiple_of((place ^ hop_to) * TOK_HALF, TOK_HALF), TOK_HALF)
            stud_out[rows, :] = piece[i * TOK_HALF : (i + 1) * TOK_HALF, :]
        if hop:
            offsets = offsets + hops
    stud = stud_out[...]
    weights_ref[...] = 1.0 / jnp.sum(col_sums_ref[...], axis=0)
    totals = [jnp.zeros((8, LANES), F32)] * TROWS
    for i in range(PRO // PRO_BLOCK):
        proto_ref, expz_ref = protos[i // NY], expzs[i // NY]
        rows = slice(i % NY * PRO_BLOCK, (i % NY + 1) * PRO_BLOCK)
        logits = lax.dot_general(
            proto_ref[rows, :], stud, CONTRACT_LAST, preferred_element_type=F32
        )
        expz = jnp.exp2(logits * (LOG2E / TEMP_STUDENT))
        expz_ref[rows, :] = expz
        for j in range(TROWS):
            part = expz[:, j * LANES : (j + 1) * LANES]
            totals[j] = totals[j] + jnp.sum(part.reshape(PRO_BLOCK // 8, 8, LANES), axis=0)
    stud_sums = [jnp.sum(t, axis=0, keepdims=True) for t in totals]
    sums = jnp.concatenate([row_sums(expos, weights_ref)] + stud_sums, axis=0).astype(BF16)
    for peer in range(PGROUP):
        sums_ref[peer] = sums


def grad_kernel(tasks, col_sums_ref, row_sums_ref, stud_ref, *refs):
    expos, expzs, outs, weights_ref = refs[:2], refs[2:4], refs[4:-1], refs[-1]
    core = lax.axis_index("core")
    weights_ref[...] = 1.0 / jnp.sum(col_sums_ref[...], axis=0)
    totals = jnp.sum(row_sums_ref[...].astype(F32), axis=0)
    target_scale = SCALE / totals[:TROWS]
    prob_scale = SCALE / totals[TROWS:]
    stud = stud_ref[...]
    for (which, step), out_ref in zip(tasks, outs):
        expo_ref, expz_ref = expos[which], expzs[which]
        base = own_first(core, which) * HROWS
        group = lax.rem(lax.axis_index("y") + step, NY) * (PRO_BLOCK // LANES)
        parts = []
        for k in range(PRO_BLOCK // LANES):
            wide = to_cols(weights_ref[pl.ds(base + group + k, 1), :])
            rows = pl.ds(pl.multiple_of((group + k) * LANES, LANES), LANES)
            cols = []
            for j in range(TROWS):
                lanes = slice(j * LANES, (j + 1) * LANES)
                target = (expo_ref[rows, lanes] * wide) * target_scale[j : j + 1, :]
                prob = expz_ref[rows, lanes] * prob_scale[j : j + 1, :]
                cols.append((prob - target).astype(BF16))
            parts.append(jnp.concatenate(cols, axis=1))
        grads = jnp.concatenate(parts, axis=0)
        out_ref[...] = jnp.dot(grads, stud, preferred_element_type=F32)


def call(kernel, out_shape, *args, scratch=(), specs=None, out_specs=None):
    return pl.pallas_call(
        kernel,
        out_shape=out_shape,
        in_specs=specs or [VMEM] * len(args),
        out_specs=out_specs or jax.tree.map(lambda _: VMEM, out_shape),
        scratch_shapes=scratch,
        compiler_params=PARAMS,
    )(*args)


def shift(x, axis, size, step):
    return lax.ppermute(x, axis, [(i, (i + step) % size) for i in range(size)])


def shards(teacher_feats, student_feats, prototypes):
    struct = jax.ShapeDtypeStruct
    near = [prototypes] + [shift(prototypes, "y", NY, step) for step in range(1, NY)]
    half = pltpu.VMEM((TOK_HALF, K), BF16)
    teach, stud, near[0] = call(
        norm_kernel,
        (
            struct((NZ, TOK_HALF, K), BF16),
            struct((TOK_HALF, K), BF16),
            struct((PRO_BLOCK, K), BF16),
        ),
        *[
            pltpu.with_memory_space_constraint(x, pltpu.HBM)
            for x in (teacher_feats, student_feats, prototypes)
        ],
        scratch=(half, half, pltpu.SemaphoreType.DMA((3 + NZ,))),
        specs=[ANY] * 3,
        out_specs=(ANY, VMEM, VMEM),
    )
    teach = lax.all_to_all(teach, "z", 0, 0, tiled=True)
    teach, stud = lax.optimization_barrier((teach, stud))
    far = [shift(proto, "core", NC, 1) for proto in near]

    col_shape = struct((TGROUP, PROWS, LANES), F32)
    row_shape = struct((PGROUP, TROWS, LANES), BF16)
    weights = pltpu.VMEM((PROWS, LANES), F32)

    square = pltpu.VMEM((HALF, TOK), F32)
    unit_shape = struct((HALF, K), BF16)
    half_sums = struct((HROWS, LANES), F32)
    near_expo, near, near_sums = call(
        teacher_kernel, (square, unit_shape, half_sums), teach, *near
    )
    far_expo, far, cols = call(
        second_teacher_kernel,
        (square, unit_shape, col_shape),
        teach,
        *far,
        near_sums,
        scratch=(pltpu.VMEM((HROWS, LANES), F32),),
    )
    pieces = [stud]
    held = stud
    for step, hop in enumerate((4, 2, 1)):
        if step:
            cols, held = lax.optimization_barrier((cols, held))
        got = lax.ppermute(held, "z", [(i, i ^ hop) for i in range(NZ)])
        cols = lax.all_to_all(cols, ("y", "core"), 0, 0, tiled=True)
        pieces.append(got)
        if step + 1 < ITERS:
            rows = call(
                row_kernel, row_shape, cols, pinned(near_expo), pinned(far_expo), scratch=(weights,)
            )
            held = jnp.concatenate(pieces, axis=0)
            rows, held = lax.optimization_barrier((rows, held))
            rows = lax.all_to_all(rows, ("z", "x"), 0, 0, tiled=True)
            cols = call(col_kernel, col_shape, rows, pinned(near_expo), pinned(far_expo))
    near_expz, far_expz, stud, rows = call(
        last_row_kernel,
        (
            square,
            square,
            struct((TOK, K), BF16),
            struct((PGROUP, 2 * TROWS, LANES), BF16),
        ),
        *pieces,
        cols,
        near,
        far,
        pinned(near_expo),
        pinned(far_expo),
        scratch=(weights,),
    )
    rows = lax.all_to_all(rows, ("z", "x"), 0, 0, tiled=True)

    def grad(*tasks, after=()):
        sums, _ = lax.optimization_barrier((rows, after))
        return call(
            functools.partial(grad_kernel, tasks),
            (struct((PRO_BLOCK, K), F32),) * len(tasks),
            cols,
            sums,
            stud,
            *[pinned(x) for x in (near_expo, far_expo, near_expz, far_expz)],
            scratch=(weights,),
        )

    def swap(part):
        return shift(part, "core", NC, 1)

    def merge(near, far):
        return (near + swap(far)).astype(BF16)

    (far2,) = grad((1, 2))
    near2, far1, far3 = grad((0, 2), (1, 1), (1, 3), after=far2)
    parts = [merge(near2, far2)]
    near1, near3, near0, far0 = grad((0, 1), (0, 3), (0, 0), (1, 0), after=parts)
    parts += [merge(near1, far1), merge(near3, far3)]
    total = near0 + swap(far0)
    for part, step in zip(parts, (2, 1, 3)):
        total = total + shift(part, "y", NY, step).astype(F32)
    return total


def solution(mesh):
    grid = Mesh(mesh.devices.reshape(NZ, NY, NX, NC), ("z", "y", "x", "core"))
    tokens = P(("z", "y"), None)
    protos = P(("z", "y", "x", "core"), None)
    return jax.shard_map(
        shards, mesh=grid, in_specs=(tokens, tokens, protos), out_specs=protos, check_vma=False
    )
```

```python
import functools
import math

import jax
import jax.numpy as jnp
from jax import lax
from jax.experimental import pallas as pl
from jax.experimental.pallas import tpu as pltpu
from jax.sharding import Mesh, PartitionSpec as P

K = 384
PROTO = 65536
TOKENS = 8192
ITERS = 3
TEMP_TEACHER = 0.07
TEMP_STUDENT = 0.1
LOG2E = math.log2(math.e)
SCALE = PROTO / (TEMP_STUDENT * math.sqrt(TOKENS))

NZ, NY, NX, NC = 8, 4, 4, 2
TOK_BLOCK = TOKENS // (NZ * NY)
TOK_HALF = TOK_BLOCK // NC
PRO_BLOCK = PROTO // (NZ * NY * NX * NC)
TOK = TOK_HALF * NZ
PRO = PRO_BLOCK * NY * NC
HALF = PRO // 2
LANES = 128
TROWS = TOK // LANES
PROWS = PRO // LANES
HROWS = HALF // LANES
TGROUP = NY * NC
PGROUP = NZ * NX

F32 = jnp.float32
BF16 = jnp.bfloat16
VMEM = pl.BlockSpec(memory_space=pltpu.VMEM)
ANY = pl.BlockSpec(memory_space=pl.ANY)
PARAMS = pltpu.CompilerParams(vmem_limit_bytes=24 * 1024 * 1024)
CONTRACT_LAST = (((1,), (1,)), ((), ()))


def pinned(x):
    return pltpu.with_memory_space_constraint(x, pltpu.VMEM)


def unit(values):
    wide = values.astype(F32)
    return (wide * lax.rsqrt(jnp.sum(wide * wide, axis=1, keepdims=True) + 1e-06)).astype(BF16)


def norm_kernel(teach_hbm, stud_hbm, proto_hbm, teach_out, stud_out, proto_out, teach_buf, stud_buf, sems):
    half = pl.ds(pl.multiple_of(lax.axis_index("core") * TOK_HALF, TOK_HALF), TOK_HALF)
    copies = [
        pltpu.make_async_copy(teach_hbm.at[half, :], teach_buf, sems.at[0]),
        pltpu.make_async_copy(stud_hbm.at[half, :], stud_buf, sems.at[1]),
        pltpu.make_async_copy(proto_hbm, proto_out, sems.at[2]),
    ]
    for copy in copies:
        copy.start()
    copies[0].wait()
    teach_buf[...] = unit(teach_buf[...])
    spread = [pltpu.make_async_copy(teach_buf, teach_out.at[z], sems.at[3 + z]) for z in range(NZ)]
    for copy in spread:
        copy.start()
    copies[1].wait()
    stud_out[...] = unit(stud_buf[...])
    copies[2].wait()
    for copy in spread:
        copy.wait()


def to_rows(values):
    return jnp.sum(values.T, axis=0, keepdims=True)


def to_cols(row):
    return jnp.broadcast_to(row, (LANES, LANES)).T


def own_first(core, which):
    return core if which == 0 else 1 - core


def block_row(step):
    place = lax.rem(lax.axis_index("y") + (NY - step), NY)
    return pl.multiple_of(place * PRO_BLOCK, PRO_BLOCK)


def teacher_kernel(teach_ref, *refs):
    raw, (expo_ref, unit_ref, sums_ref) = refs[:NY], refs[NY:]
    teach = teach_ref[...].reshape(TOK, K)
    for step in range(NY):
        base = block_row(step)
        rows = pl.ds(base, PRO_BLOCK)
        proto = unit(raw[step][...])
        unit_ref[rows, :] = proto
        logits = lax.dot_general(proto, teach, CONTRACT_LAST, preferred_element_type=F32)
        expo = jnp.exp2(logits * (LOG2E / TEMP_TEACHER))
        expo_ref[rows, :] = expo
        total = sum(expo[:, j * LANES : (j + 1) * LANES] for j in range(TROWS))
        for k in range(PRO_BLOCK // LANES):
            sums_ref[pl.ds(base // LANES + k, 1), :] = to_rows(total[k * LANES : (k + 1) * LANES, :])


def second_teacher_kernel(teach_ref, *refs):
    raw, first_ref, (expo_ref, unit_ref, sums_ref, second_ref) = refs[:NY], refs[NY], refs[NY + 1 :]
    teacher_kernel(teach_ref, *raw, expo_ref, unit_ref, second_ref)
    core = lax.axis_index("core")
    for peer in range(TGROUP):
        for which, part_ref in enumerate((first_ref, second_ref)):
            base = pl.multiple_of(own_first(core, which) * HROWS, HROWS)
            sums_ref[peer, pl.ds(base, HROWS), :] = part_ref[...]


def col_sums(expo_refs, weights, sums_ref):
    core = lax.axis_index("core")
    for which, expo_ref in enumerate(expo_refs):
        base = own_first(core, which) * HROWS

        def group(i, carry):
            rows = pl.ds(pl.multiple_of(i * LANES, LANES), LANES)
            total = None
            for j in range(TROWS):
                term = expo_ref[rows, j * LANES : (j + 1) * LANES] * weights[j : j + 1, :]
                total = term if total is None else total + term
            sums_ref[0, pl.ds(base + i, 1), :] = to_rows(total)
            return carry

        lax.fori_loop(0, HROWS, group, 0, unroll=True)
    for peer in range(1, TGROUP):
        sums_ref[peer] = sums_ref[0]


def col_kernel(row_sums_ref, first_ref, second_ref, sums_ref):
    weights = 1.0 / jnp.sum(row_sums_ref[...].astype(F32), axis=0)
    col_sums((first_ref, second_ref), weights, sums_ref)


def row_sums(expo_refs, weights_ref):
    core = lax.axis_index("core")
    totals = (jnp.zeros((8, LANES), F32),) * TROWS
    for which, expo_ref in enumerate(expo_refs):
        base = own_first(core, which) * HROWS

        def group(i, totals):
            rows = pl.ds(pl.multiple_of(i * LANES, LANES), LANES)
            wide = to_cols(weights_ref[pl.ds(base + i, 1), :])
            out = []
            for j in range(TROWS):
                term = expo_ref[rows, j * LANES : (j + 1) * LANES] * wide
                out.append(totals[j] + jnp.sum(term.reshape(LANES // 8, 8, LANES), axis=0))
            return tuple(out)

        totals = lax.fori_loop(0, HROWS, group, totals, unroll=True)
    return jnp.concatenate([jnp.sum(t, axis=0, keepdims=True) for t in totals], axis=0)


def row_kernel(col_sums_ref, first_ref, second_ref, sums_ref, weights_ref):
    weights_ref[...] = 1.0 / jnp.sum(col_sums_ref[...], axis=0)
    sums = row_sums((first_ref, second_ref), weights_ref).astype(BF16)
    for peer in range(PGROUP):
        sums_ref[peer] = sums


def last_row_kernel(*refs):
    pieces, (col_sums_ref, *protos), expos, outs = refs[:4], refs[4:7], refs[7:9], refs[9:]
    *expzs, stud_out, sums_ref, weights_ref = outs
    place = lax.axis_index("z")
    offsets = [0]
    for piece, hop in zip(pieces, (0, 4, 2, 1)):
        hops = [o ^ hop for o in offsets]
        for i, hop_to in enumerate(hops):
            rows = pl.ds(pl.multiple_of((place ^ hop_to) * TOK_HALF, TOK_HALF), TOK_HALF)
            stud_out[rows, :] = piece[i * TOK_HALF : (i + 1) * TOK_HALF, :]
        if hop:
            offsets = offsets + hops
    stud = stud_out[...]
    weights_ref[...] = 1.0 / jnp.sum(col_sums_ref[...], axis=0)
    totals = [jnp.zeros((8, LANES), F32)] * TROWS
    for i in range(PRO // PRO_BLOCK):
        proto_ref, expz_ref = protos[i // NY], expzs[i // NY]
        rows = slice(i % NY * PRO_BLOCK, (i % NY + 1) * PRO_BLOCK)
        logits = lax.dot_general(
            proto_ref[rows, :], stud, CONTRACT_LAST, preferred_element_type=F32
        )
        expz = jnp.exp2(logits * (LOG2E / TEMP_STUDENT))
        expz_ref[rows, :] = expz
        for j in range(TROWS):
            part = expz[:, j * LANES : (j + 1) * LANES]
            totals[j] = totals[j] + jnp.sum(part.reshape(PRO_BLOCK // 8, 8, LANES), axis=0)
    stud_sums = [jnp.sum(t, axis=0, keepdims=True) for t in totals]
    sums = jnp.concatenate([row_sums(expos, weights_ref)] + stud_sums, axis=0).astype(BF16)
    for peer in range(PGROUP):
        sums_ref[peer] = sums


def grad_kernel(tasks, col_sums_ref, row_sums_ref, stud_ref, *refs):
    expos, expzs, outs, weights_ref = refs[:2], refs[2:4], refs[4:-1], refs[-1]
    core = lax.axis_index("core")
    weights_ref[...] = 1.0 / jnp.sum(col_sums_ref[...], axis=0)
    totals = jnp.sum(row_sums_ref[...].astype(F32), axis=0)
    target_scale = SCALE / totals[:TROWS]
    prob_scale = SCALE / totals[TROWS:]
    stud = stud_ref[...]
    for (which, step), out_ref in zip(tasks, outs):
        expo_ref, expz_ref = expos[which], expzs[which]
        base = own_first(core, which) * HROWS
        group = lax.rem(lax.axis_index("y") + step, NY) * (PRO_BLOCK // LANES)
        parts = []
        for k in range(PRO_BLOCK // LANES):
            wide = to_cols(weights_ref[pl.ds(base + group + k, 1), :])
            rows = pl.ds(pl.multiple_of((group + k) * LANES, LANES), LANES)
            cols = []
            for j in range(TROWS):
                lanes = slice(j * LANES, (j + 1) * LANES)
                target = (expo_ref[rows, lanes] * wide) * target_scale[j : j + 1, :]
                prob = expz_ref[rows, lanes] * prob_scale[j : j + 1, :]
                cols.append((prob - target).astype(BF16))
            parts.append(jnp.concatenate(cols, axis=1))
        grads = jnp.concatenate(parts, axis=0)
        out_ref[...] = jnp.dot(grads, stud, preferred_element_type=F32)


def call(kernel, out_shape, *args, scratch=(), specs=None, out_specs=None):
    return pl.pallas_call(
        kernel,
        out_shape=out_shape,
        in_specs=specs or [VMEM] * len(args),
        out_specs=out_specs or jax.tree.map(lambda _: VMEM, out_shape),
        scratch_shapes=scratch,
        compiler_params=PARAMS,
    )(*args)


def shift(x, axis, size, step):
    return lax.ppermute(x, axis, [(i, (i + step) % size) for i in range(size)])


def shards(teacher_feats, student_feats, prototypes):
    struct = jax.ShapeDtypeStruct
    near = [prototypes] + [shift(prototypes, "y", NY, step) for step in range(1, NY)]
    half = pltpu.VMEM((TOK_HALF, K), BF16)
    teach, stud, near[0] = call(
        norm_kernel,
        (
            struct((NZ, TOK_HALF, K), BF16),
            struct((TOK_HALF, K), BF16),
            struct((PRO_BLOCK, K), BF16),
        ),
        *[
            pltpu.with_memory_space_constraint(x, pltpu.HBM)
            for x in (teacher_feats, student_feats, prototypes)
        ],
        scratch=(half, half, pltpu.SemaphoreType.DMA((3 + NZ,))),
        specs=[ANY] * 3,
        out_specs=(ANY, VMEM, VMEM),
    )
    teach = lax.all_to_all(teach, "z", 0, 0, tiled=True)
    got = lax.ppermute(stud, "z", [(i, i ^ 4) for i in range(NZ)])
    far = [shift(proto, "core", NC, 1) for proto in near]

    col_shape = struct((TGROUP, PROWS, LANES), F32)
    row_shape = struct((PGROUP, TROWS, LANES), BF16)
    weights = pltpu.VMEM((PROWS, LANES), F32)

    square = pltpu.VMEM((HALF, TOK), F32)
    unit_shape = struct((HALF, K), BF16)
    half_sums = struct((HROWS, LANES), F32)
    near_expo, near, near_sums = call(
        teacher_kernel, (square, unit_shape, half_sums), teach, *near
    )
    far_expo, far, cols = call(
        second_teacher_kernel,
        (square, unit_shape, col_shape),
        teach,
        *far,
        near_sums,
        scratch=(pltpu.VMEM((HROWS, LANES), F32),),
    )
    cols, got = lax.optimization_barrier((cols, got))
    pieces = [stud]
    for step, hop in enumerate((4, 2, 1)):
        if step:
            cols, held = lax.optimization_barrier((cols, held))
            got = lax.ppermute(held, "z", [(i, i ^ hop) for i in range(NZ)])
        cols = lax.all_to_all(cols, ("y", "core"), 0, 0, tiled=True)
        if step == 0:
            cols, got = lax.optimization_barrier((cols, got))
        pieces.append(got)
        if step + 1 < ITERS:
            rows = call(
                row_kernel, row_shape, cols, pinned(near_expo), pinned(far_expo), scratch=(weights,)
            )
            held = jnp.concatenate(pieces, axis=0)
            rows, held = lax.optimization_barrier((rows, held))
            rows = lax.all_to_all(rows, ("z", "x"), 0, 0, tiled=True)
            cols = call(col_kernel, col_shape, rows, pinned(near_expo), pinned(far_expo))
    near_expz, far_expz, stud, rows = call(
        last_row_kernel,
        (
            square,
            square,
            struct((TOK, K), BF16),
            struct((PGROUP, 2 * TROWS, LANES), BF16),
        ),
        *pieces,
        cols,
        near,
        far,
        pinned(near_expo),
        pinned(far_expo),
        scratch=(weights,),
    )
    rows = lax.all_to_all(rows, ("z", "x"), 0, 0, tiled=True)

    def grad(*tasks, after=()):
        sums, _ = lax.optimization_barrier((rows, after))
        return call(
            functools.partial(grad_kernel, tasks),
            (struct((PRO_BLOCK, K), F32),) * len(tasks),
            cols,
            sums,
            stud,
            *[pinned(x) for x in (near_expo, far_expo, near_expz, far_expz)],
            scratch=(weights,),
        )

    def swap(part):
        return shift(part, "core", NC, 1)

    def merge(near, far):
        return (near + swap(far)).astype(BF16)

    (far2,) = grad((1, 2))
    near2, far1, far3 = grad((0, 2), (1, 1), (1, 3), after=far2)
    parts = [merge(near2, far2)]
    near1, near3, near0, far0 = grad((0, 1), (0, 3), (0, 0), (1, 0), after=parts)
    parts += [merge(near1, far1), merge(near3, far3)]
    total = near0 + swap(far0)
    for part, step in zip(parts, (2, 1, 3)):
        total = total + shift(part, "y", NY, step).astype(F32)
    return total


def solution(mesh):
    grid = Mesh(mesh.devices.reshape(NZ, NY, NX, NC), ("z", "y", "x", "core"))
    tokens = P(("z", "y"), None)
    protos = P(("z", "y", "x", "core"), None)
    return jax.shard_map(
        shards, mesh=grid, in_specs=(tokens, tokens, protos), out_specs=protos, check_vma=False
    )
```

```python
import functools
import math

import jax
import jax.numpy as jnp
from jax import lax
from jax.experimental import pallas as pl
from jax.experimental.pallas import tpu as pltpu
from jax.sharding import Mesh, PartitionSpec as P

K = 384
PROTO = 65536
TOKENS = 8192
ITERS = 3
TEMP_TEACHER = 0.07
TEMP_STUDENT = 0.1
LOG2E = math.log2(math.e)
SCALE = PROTO / (TEMP_STUDENT * math.sqrt(TOKENS))

NZ, NY, NX, NC = 8, 4, 4, 2
TOK_BLOCK = TOKENS // (NZ * NY)
TOK_HALF = TOK_BLOCK // NC
PRO_BLOCK = PROTO // (NZ * NY * NX * NC)
TOK = TOK_HALF * NZ
PRO = PRO_BLOCK * NY * NC
HALF = PRO // 2
LANES = 128
TROWS = TOK // LANES
PROWS = PRO // LANES
HROWS = HALF // LANES
TGROUP = NY * NC
PGROUP = NZ * NX

F32 = jnp.float32
BF16 = jnp.bfloat16
VMEM = pl.BlockSpec(memory_space=pltpu.VMEM)
ANY = pl.BlockSpec(memory_space=pl.ANY)
PARAMS = pltpu.CompilerParams(vmem_limit_bytes=24 * 1024 * 1024)
CONTRACT_LAST = (((1,), (1,)), ((), ()))


def pinned(x):
    return pltpu.with_memory_space_constraint(x, pltpu.VMEM)


def unit(values):
    wide = values.astype(F32)
    return (wide * lax.rsqrt(jnp.sum(wide * wide, axis=1, keepdims=True) + 1e-06)).astype(BF16)


def norm_kernel(teach_hbm, stud_hbm, proto_hbm, teach_out, stud_out, proto_out, teach_buf, stud_buf, sems):
    half = pl.ds(pl.multiple_of(lax.axis_index("core") * TOK_HALF, TOK_HALF), TOK_HALF)
    copies = [
        pltpu.make_async_copy(teach_hbm.at[half, :], teach_buf, sems.at[0]),
        pltpu.make_async_copy(stud_hbm.at[half, :], stud_buf, sems.at[1]),
        pltpu.make_async_copy(proto_hbm, proto_out, sems.at[2]),
    ]
    for copy in copies:
        copy.start()
    copies[0].wait()
    teach_buf[...] = unit(teach_buf[...])
    spread = [pltpu.make_async_copy(teach_buf, teach_out.at[z], sems.at[3 + z]) for z in range(NZ)]
    for copy in spread:
        copy.start()
    copies[1].wait()
    stud_out[...] = unit(stud_buf[...])
    copies[2].wait()
    for copy in spread:
        copy.wait()


def to_rows(values):
    return jnp.sum(values.T, axis=0, keepdims=True)


def to_cols(row):
    return jnp.broadcast_to(row, (LANES, LANES)).T


def own_first(core, which):
    return core if which == 0 else 1 - core


def block_row(step):
    place = lax.rem(lax.axis_index("y") + (NY - step), NY)
    return pl.multiple_of(place * PRO_BLOCK, PRO_BLOCK)


def teacher_kernel(teach_ref, *refs):
    raw, (expo_ref, unit_ref, sums_ref) = refs[:NY], refs[NY:]
    teach = teach_ref[...].reshape(TOK, K)
    for step in range(NY):
        base = block_row(step)
        rows = pl.ds(base, PRO_BLOCK)
        proto = unit(raw[step][...])
        unit_ref[rows, :] = proto
        logits = lax.dot_general(proto, teach, CONTRACT_LAST, preferred_element_type=F32)
        expo = jnp.exp2(logits * (LOG2E / TEMP_TEACHER))
        expo_ref[rows, :] = expo
        total = sum(expo[:, j * LANES : (j + 1) * LANES] for j in range(TROWS))
        for k in range(PRO_BLOCK // LANES):
            sums_ref[pl.ds(base // LANES + k, 1), :] = to_rows(total[k * LANES : (k + 1) * LANES, :])


def second_teacher_kernel(teach_ref, *refs):
    raw, first_ref, (expo_ref, unit_ref, sums_ref, second_ref) = refs[:NY], refs[NY], refs[NY + 1 :]
    teacher_kernel(teach_ref, *raw, expo_ref, unit_ref, second_ref)
    core = lax.axis_index("core")
    for peer in range(TGROUP):
        for which, part_ref in enumerate((first_ref, second_ref)):
            base = pl.multiple_of(own_first(core, which) * HROWS, HROWS)
            sums_ref[peer, pl.ds(base, HROWS), :] = part_ref[...]


def col_sums(expo_refs, weights, sums_ref):
    core = lax.axis_index("core")
    for which, expo_ref in enumerate(expo_refs):
        base = own_first(core, which) * HROWS

        def group(i, carry):
            rows = pl.ds(pl.multiple_of(i * LANES, LANES), LANES)
            total = None
            for j in range(TROWS):
                term = expo_ref[rows, j * LANES : (j + 1) * LANES] * weights[j : j + 1, :]
                total = term if total is None else total + term
            sums_ref[0, pl.ds(base + i, 1), :] = to_rows(total)
            return carry

        lax.fori_loop(0, HROWS, group, 0, unroll=True)
    for peer in range(1, TGROUP):
        sums_ref[peer] = sums_ref[0]


def col_kernel(row_sums_ref, first_ref, second_ref, sums_ref):
    weights = 1.0 / jnp.sum(row_sums_ref[...].astype(F32), axis=0)
    col_sums((first_ref, second_ref), weights, sums_ref)


def row_sums(expo_refs, weights_ref):
    core = lax.axis_index("core")
    totals = (jnp.zeros((8, LANES), F32),) * TROWS
    for which, expo_ref in enumerate(expo_refs):
        base = own_first(core, which) * HROWS

        def group(i, totals):
            rows = pl.ds(pl.multiple_of(i * LANES, LANES), LANES)
            wide = to_cols(weights_ref[pl.ds(base + i, 1), :])
            out = []
            for j in range(TROWS):
                term = expo_ref[rows, j * LANES : (j + 1) * LANES] * wide
                out.append(totals[j] + jnp.sum(term.reshape(LANES // 8, 8, LANES), axis=0))
            return tuple(out)

        totals = lax.fori_loop(0, HROWS, group, totals, unroll=True)
    return jnp.concatenate([jnp.sum(t, axis=0, keepdims=True) for t in totals], axis=0)


def row_kernel(col_sums_ref, first_ref, second_ref, sums_ref, weights_ref):
    weights_ref[...] = 1.0 / jnp.sum(col_sums_ref[...], axis=0)
    sums = row_sums((first_ref, second_ref), weights_ref).astype(BF16)
    for peer in range(PGROUP):
        sums_ref[peer] = sums


def last_row_kernel(*refs):
    pieces, (col_sums_ref, *protos), expos, outs = refs[:4], refs[4:7], refs[7:9], refs[9:]
    *expzs, stud_out, sums_ref, weights_ref = outs
    place = lax.axis_index("z")
    offsets = [0]
    for piece, hop in zip(pieces, (0, 4, 2, 1)):
        hops = [o ^ hop for o in offsets]
        for i, hop_to in enumerate(hops):
            rows = pl.ds(pl.multiple_of((place ^ hop_to) * TOK_HALF, TOK_HALF), TOK_HALF)
            stud_out[rows, :] = piece[i * TOK_HALF : (i + 1) * TOK_HALF, :]
        if hop:
            offsets = offsets + hops
    stud = stud_out[...]
    weights_ref[...] = 1.0 / jnp.sum(col_sums_ref[...], axis=0)
    totals = [jnp.zeros((8, LANES), F32)] * TROWS
    for i in range(PRO // PRO_BLOCK):
        proto_ref, expz_ref = protos[i // NY], expzs[i // NY]
        rows = slice(i % NY * PRO_BLOCK, (i % NY + 1) * PRO_BLOCK)
        logits = lax.dot_general(
            proto_ref[rows, :], stud, CONTRACT_LAST, preferred_element_type=F32
        )
        expz = jnp.exp2(logits * (LOG2E / TEMP_STUDENT))
        expz_ref[rows, :] = expz
        for j in range(TROWS):
            part = expz[:, j * LANES : (j + 1) * LANES]
            totals[j] = totals[j] + jnp.sum(part.reshape(PRO_BLOCK // 8, 8, LANES), axis=0)
    stud_sums = [jnp.sum(t, axis=0, keepdims=True) for t in totals]
    sums = jnp.concatenate([row_sums(expos, weights_ref)] + stud_sums, axis=0).astype(BF16)
    for peer in range(PGROUP):
        sums_ref[peer] = sums


def grad_kernel(tasks, col_sums_ref, row_sums_ref, stud_ref, *refs):
    expos, expzs, outs, weights_ref = refs[:2], refs[2:4], refs[4:-1], refs[-1]
    core = lax.axis_index("core")
    weights_ref[...] = 1.0 / jnp.sum(col_sums_ref[...], axis=0)
    totals = jnp.sum(row_sums_ref[...].astype(F32), axis=0)
    target_scale = SCALE / totals[:TROWS]
    prob_scale = SCALE / totals[TROWS:]
    stud = stud_ref[...]
    for (which, step), out_ref in zip(tasks, outs):
        expo_ref, expz_ref = expos[which], expzs[which]
        base = own_first(core, which) * HROWS
        group = lax.rem(lax.axis_index("y") + step, NY) * (PRO_BLOCK // LANES)
        parts = []
        for k in range(PRO_BLOCK // LANES):
            wide = to_cols(weights_ref[pl.ds(base + group + k, 1), :])
            rows = pl.ds(pl.multiple_of((group + k) * LANES, LANES), LANES)
            cols = []
            for j in range(TROWS):
                lanes = slice(j * LANES, (j + 1) * LANES)
                target = (expo_ref[rows, lanes] * wide) * target_scale[j : j + 1, :]
                prob = expz_ref[rows, lanes] * prob_scale[j : j + 1, :]
                cols.append((prob - target).astype(BF16))
            parts.append(jnp.concatenate(cols, axis=1))
        grads = jnp.concatenate(parts, axis=0)
        out_ref[...] = jnp.dot(grads, stud, preferred_element_type=F32)


def call(kernel, out_shape, *args, scratch=(), specs=None, out_specs=None):
    return pl.pallas_call(
        kernel,
        out_shape=out_shape,
        in_specs=specs or [VMEM] * len(args),
        out_specs=out_specs or jax.tree.map(lambda _: VMEM, out_shape),
        scratch_shapes=scratch,
        compiler_params=PARAMS,
    )(*args)


def shift(x, axis, size, step):
    return lax.ppermute(x, axis, [(i, (i + step) % size) for i in range(size)])


def shards(teacher_feats, student_feats, prototypes):
    struct = jax.ShapeDtypeStruct
    near = [prototypes] + [shift(prototypes, "y", NY, step) for step in range(1, NY)]
    half = pltpu.VMEM((TOK_HALF, K), BF16)
    teach, stud, near[0] = call(
        norm_kernel,
        (
            struct((NZ, TOK_HALF, K), BF16),
            struct((TOK_HALF, K), BF16),
            struct((PRO_BLOCK, K), BF16),
        ),
        *[
            pltpu.with_memory_space_constraint(x, pltpu.HBM)
            for x in (teacher_feats, student_feats, prototypes)
        ],
        scratch=(half, half, pltpu.SemaphoreType.DMA((3 + NZ,))),
        specs=[ANY] * 3,
        out_specs=(ANY, VMEM, VMEM),
    )
    teach = lax.all_to_all(teach, "z", 0, 0, tiled=True)
    got = lax.ppermute(stud, "z", [(i, i ^ 4) for i in range(NZ)])
    far = [shift(proto, "core", NC, 1) for proto in near]

    col_shape = struct((TGROUP, PROWS, LANES), F32)
    row_shape = struct((PGROUP, TROWS, LANES), BF16)
    weights = pltpu.VMEM((PROWS, LANES), F32)

    square = pltpu.VMEM((HALF, TOK), F32)
    unit_shape = struct((HALF, K), BF16)
    half_sums = struct((HROWS, LANES), F32)
    near_expo, near, near_sums = call(
        teacher_kernel, (square, unit_shape, half_sums), teach, *near
    )
    far_expo, far, cols = call(
        second_teacher_kernel,
        (square, unit_shape, col_shape),
        teach,
        *far,
        near_sums,
        scratch=(pltpu.VMEM((HROWS, LANES), F32),),
    )
    pieces = [stud, got]
    for step in range(ITERS):
        if step + 1 < ITERS:
            cols, pieces = lax.optimization_barrier((cols, pieces))
            held = jnp.concatenate(pieces, axis=0)
            cols, held = lax.optimization_barrier((cols, held))
            hop = (2, 1)[step]
            got = lax.ppermute(held, "z", [(i, i ^ hop) for i in range(NZ)])
        cols = lax.all_to_all(cols, ("y", "core"), 0, 0, tiled=True)
        if step + 1 < ITERS:
            pieces = pieces + [got]
            rows = call(
                row_kernel, row_shape, cols, pinned(near_expo), pinned(far_expo), scratch=(weights,)
            )
            rows = lax.all_to_all(rows, ("z", "x"), 0, 0, tiled=True)
            cols = call(col_kernel, col_shape, rows, pinned(near_expo), pinned(far_expo))
    near_expz, far_expz, stud, rows = call(
        last_row_kernel,
        (
            square,
            square,
            struct((TOK, K), BF16),
            struct((PGROUP, 2 * TROWS, LANES), BF16),
        ),
        *pieces,
        cols,
        near,
        far,
        pinned(near_expo),
        pinned(far_expo),
        scratch=(weights,),
    )
    rows = lax.all_to_all(rows, ("z", "x"), 0, 0, tiled=True)

    def grad(*tasks, after=()):
        sums, _ = lax.optimization_barrier((rows, after))
        return call(
            functools.partial(grad_kernel, tasks),
            (struct((PRO_BLOCK, K), F32),) * len(tasks),
            cols,
            sums,
            stud,
            *[pinned(x) for x in (near_expo, far_expo, near_expz, far_expz)],
            scratch=(weights,),
        )

    def swap(part):
        return shift(part, "core", NC, 1)

    def merge(near, far):
        return (near + swap(far)).astype(BF16)

    (far2,) = grad((1, 2))
    near2, far1, far3 = grad((0, 2), (1, 1), (1, 3), after=far2)
    parts = [merge(near2, far2)]
    near1, near3, near0, far0 = grad((0, 1), (0, 3), (0, 0), (1, 0), after=parts)
    parts += [merge(near1, far1), merge(near3, far3)]
    total = near0 + swap(far0)
    for part, step in zip(parts, (2, 1, 3)):
        total = total + shift(part, "y", NY, step).astype(F32)
    return total


def solution(mesh):
    grid = Mesh(mesh.devices.reshape(NZ, NY, NX, NC), ("z", "y", "x", "core"))
    tokens = P(("z", "y"), None)
    protos = P(("z", "y", "x", "core"), None)
    return jax.shard_map(
        shards, mesh=grid, in_specs=(tokens, tokens, protos), out_specs=protos, check_vma=False
    )
```

```python
import functools
import math

import jax
import jax.numpy as jnp
from jax import lax
from jax.experimental import pallas as pl
from jax.experimental.pallas import tpu as pltpu
from jax.sharding import Mesh, PartitionSpec as P

K = 384
PROTO = 65536
TOKENS = 8192
ITERS = 3
TEMP_TEACHER = 0.07
TEMP_STUDENT = 0.1
LOG2E = math.log2(math.e)
SCALE = PROTO / (TEMP_STUDENT * math.sqrt(TOKENS))

NZ, NY, NX, NC = 8, 4, 4, 2
TOK_BLOCK = TOKENS // (NZ * NY)
TOK_HALF = TOK_BLOCK // NC
PRO_BLOCK = PROTO // (NZ * NY * NX * NC)
TOK = TOK_HALF * NZ
PRO = PRO_BLOCK * NY * NC
HALF = PRO // 2
LANES = 128
TROWS = TOK // LANES
PROWS = PRO // LANES
HROWS = HALF // LANES
TGROUP = NY * NC
PGROUP = NZ * NX

F32 = jnp.float32
BF16 = jnp.bfloat16
VMEM = pl.BlockSpec(memory_space=pltpu.VMEM)
ANY = pl.BlockSpec(memory_space=pl.ANY)
PARAMS = pltpu.CompilerParams(vmem_limit_bytes=24 * 1024 * 1024)
CONTRACT_LAST = (((1,), (1,)), ((), ()))


def pinned(x):
    return pltpu.with_memory_space_constraint(x, pltpu.VMEM)


def unit(values):
    wide = values.astype(F32)
    return (wide * lax.rsqrt(jnp.sum(wide * wide, axis=1, keepdims=True) + 1e-06)).astype(BF16)


def norm_kernel(teach_hbm, stud_hbm, proto_hbm, teach_out, stud_out, proto_out, teach_buf, stud_buf, sems):
    half = pl.ds(pl.multiple_of(lax.axis_index("core") * TOK_HALF, TOK_HALF), TOK_HALF)
    copies = [
        pltpu.make_async_copy(teach_hbm.at[half, :], teach_buf, sems.at[0]),
        pltpu.make_async_copy(stud_hbm.at[half, :], stud_buf, sems.at[1]),
        pltpu.make_async_copy(proto_hbm, proto_out, sems.at[2]),
    ]
    for copy in copies:
        copy.start()
    copies[0].wait()
    teach_buf[...] = unit(teach_buf[...])
    spread = [pltpu.make_async_copy(teach_buf, teach_out.at[z], sems.at[3 + z]) for z in range(NZ)]
    for copy in spread:
        copy.start()
    copies[1].wait()
    stud_out[...] = unit(stud_buf[...])
    copies[2].wait()
    for copy in spread:
        copy.wait()


def to_rows(values):
    return jnp.sum(values.T, axis=0, keepdims=True)


def to_cols(row):
    return jnp.broadcast_to(row, (LANES, LANES)).T


def own_first(core, which):
    return core if which == 0 else 1 - core


def block_row(step):
    place = lax.rem(lax.axis_index("y") + (NY - step), NY)
    return pl.multiple_of(place * PRO_BLOCK, PRO_BLOCK)


def teacher_kernel(teach_ref, *refs):
    raw, (expo_ref, unit_ref, sums_ref) = refs[:NY], refs[NY:]
    teach = teach_ref[...].reshape(TOK, K)
    for step in range(NY):
        base = block_row(step)
        rows = pl.ds(base, PRO_BLOCK)
        proto = unit(raw[step][...])
        unit_ref[rows, :] = proto
        logits = lax.dot_general(proto, teach, CONTRACT_LAST, preferred_element_type=F32)
        expo = jnp.exp2(logits * (LOG2E / TEMP_TEACHER))
        expo_ref[rows, :] = expo
        total = sum(expo[:, j * LANES : (j + 1) * LANES] for j in range(TROWS))
        for k in range(PRO_BLOCK // LANES):
            sums_ref[pl.ds(base // LANES + k, 1), :] = to_rows(total[k * LANES : (k + 1) * LANES, :])


def both_teacher_kernel(teach_ref, *refs):
    near, far, outs = refs[:NY], refs[NY : 2 * NY], refs[2 * NY :]
    near_ref, near_unit, far_ref, far_unit, sums_ref, near_sums, far_sums = outs
    teacher_kernel(teach_ref, *near, near_ref, near_unit, near_sums)
    teacher_kernel(teach_ref, *far, far_ref, far_unit, far_sums)
    core = lax.axis_index("core")
    for peer in range(TGROUP):
        for which, part_ref in enumerate((near_sums, far_sums)):
            base = pl.multiple_of(own_first(core, which) * HROWS, HROWS)
            sums_ref[peer, pl.ds(base, HROWS), :] = part_ref[...]


def col_sums(expo_refs, weights, sums_ref):
    core = lax.axis_index("core")
    for which, expo_ref in enumerate(expo_refs):
        base = own_first(core, which) * HROWS

        def group(i, carry):
            rows = pl.ds(pl.multiple_of(i * LANES, LANES), LANES)
            total = None
            for j in range(TROWS):
                term = expo_ref[rows, j * LANES : (j + 1) * LANES] * weights[j : j + 1, :]
                total = term if total is None else total + term
            sums_ref[0, pl.ds(base + i, 1), :] = to_rows(total)
            return carry

        lax.fori_loop(0, HROWS, group, 0, unroll=True)
    for peer in range(1, TGROUP):
        sums_ref[peer] = sums_ref[0]


def col_kernel(row_sums_ref, first_ref, second_ref, sums_ref):
    weights = 1.0 / jnp.sum(row_sums_ref[...].astype(F32), axis=0)
    col_sums((first_ref, second_ref), weights, sums_ref)


def row_sums(expo_refs, weights_ref):
    core = lax.axis_index("core")
    totals = (jnp.zeros((8, LANES), F32),) * TROWS
    for which, expo_ref in enumerate(expo_refs):
        base = own_first(core, which) * HROWS

        def group(i, totals):
            rows = pl.ds(pl.multiple_of(i * LANES, LANES), LANES)
            wide = to_cols(weights_ref[pl.ds(base + i, 1), :])
            out = []
            for j in range(TROWS):
                term = expo_ref[rows, j * LANES : (j + 1) * LANES] * wide
                out.append(totals[j] + jnp.sum(term.reshape(LANES // 8, 8, LANES), axis=0))
            return tuple(out)

        totals = lax.fori_loop(0, HROWS, group, totals, unroll=True)
    return jnp.concatenate([jnp.sum(t, axis=0, keepdims=True) for t in totals], axis=0)


def row_kernel(col_sums_ref, first_ref, second_ref, sums_ref, weights_ref):
    weights_ref[...] = 1.0 / jnp.sum(col_sums_ref[...], axis=0)
    sums = row_sums((first_ref, second_ref), weights_ref).astype(BF16)
    for peer in range(PGROUP):
        sums_ref[peer] = sums


def last_row_kernel(*refs):
    pieces, (col_sums_ref, *protos), expos, outs = refs[:4], refs[4:7], refs[7:9], refs[9:]
    *expzs, stud_out, sums_ref, weights_ref = outs
    place = lax.axis_index("z")
    offsets = [0]
    for piece, hop in zip(pieces, (0, 4, 2, 1)):
        hops = [o ^ hop for o in offsets]
        for i, hop_to in enumerate(hops):
            rows = pl.ds(pl.multiple_of((place ^ hop_to) * TOK_HALF, TOK_HALF), TOK_HALF)
            stud_out[rows, :] = piece[i * TOK_HALF : (i + 1) * TOK_HALF, :]
        if hop:
            offsets = offsets + hops
    stud = stud_out[...]
    weights_ref[...] = 1.0 / jnp.sum(col_sums_ref[...], axis=0)
    totals = [jnp.zeros((8, LANES), F32)] * TROWS
    for i in range(PRO // PRO_BLOCK):
        proto_ref, expz_ref = protos[i // NY], expzs[i // NY]
        rows = slice(i % NY * PRO_BLOCK, (i % NY + 1) * PRO_BLOCK)
        logits = lax.dot_general(
            proto_ref[rows, :], stud, CONTRACT_LAST, preferred_element_type=F32
        )
        expz = jnp.exp2(logits * (LOG2E / TEMP_STUDENT))
        expz_ref[rows, :] = expz
        for j in range(TROWS):
            part = expz[:, j * LANES : (j + 1) * LANES]
            totals[j] = totals[j] + jnp.sum(part.reshape(PRO_BLOCK // 8, 8, LANES), axis=0)
    stud_sums = [jnp.sum(t, axis=0, keepdims=True) for t in totals]
    sums = jnp.concatenate([row_sums(expos, weights_ref)] + stud_sums, axis=0).astype(BF16)
    for peer in range(PGROUP):
        sums_ref[peer] = sums


def grad_kernel(tasks, col_sums_ref, row_sums_ref, stud_ref, *refs):
    expos, expzs, outs, weights_ref = refs[:2], refs[2:4], refs[4:-1], refs[-1]
    core = lax.axis_index("core")
    weights_ref[...] = 1.0 / jnp.sum(col_sums_ref[...], axis=0)
    totals = jnp.sum(row_sums_ref[...].astype(F32), axis=0)
    target_scale = SCALE / totals[:TROWS]
    prob_scale = SCALE / totals[TROWS:]
    stud = stud_ref[...]
    for (which, step), out_ref in zip(tasks, outs):
        expo_ref, expz_ref = expos[which], expzs[which]
        base = own_first(core, which) * HROWS
        group = lax.rem(lax.axis_index("y") + step, NY) * (PRO_BLOCK // LANES)
        parts = []
        for k in range(PRO_BLOCK // LANES):
            wide = to_cols(weights_ref[pl.ds(base + group + k, 1), :])
            rows = pl.ds(pl.multiple_of((group + k) * LANES, LANES), LANES)
            cols = []
            for j in range(TROWS):
                lanes = slice(j * LANES, (j + 1) * LANES)
                target = (expo_ref[rows, lanes] * wide) * target_scale[j : j + 1, :]
                prob = expz_ref[rows, lanes] * prob_scale[j : j + 1, :]
                cols.append((prob - target).astype(BF16))
            parts.append(jnp.concatenate(cols, axis=1))
        grads = jnp.concatenate(parts, axis=0)
        out_ref[...] = jnp.dot(grads, stud, preferred_element_type=F32)


def call(kernel, out_shape, *args, scratch=(), specs=None, out_specs=None):
    return pl.pallas_call(
        kernel,
        out_shape=out_shape,
        in_specs=specs or [VMEM] * len(args),
        out_specs=out_specs or jax.tree.map(lambda _: VMEM, out_shape),
        scratch_shapes=scratch,
        compiler_params=PARAMS,
    )(*args)


def shift(x, axis, size, step):
    return lax.ppermute(x, axis, [(i, (i + step) % size) for i in range(size)])


def shards(teacher_feats, student_feats, prototypes):
    struct = jax.ShapeDtypeStruct
    near = [prototypes] + [shift(prototypes, "y", NY, step) for step in range(1, NY)]
    half = pltpu.VMEM((TOK_HALF, K), BF16)
    teach, stud, near[0] = call(
        norm_kernel,
        (
            struct((NZ, TOK_HALF, K), BF16),
            struct((TOK_HALF, K), BF16),
            struct((PRO_BLOCK, K), BF16),
        ),
        *[
            pltpu.with_memory_space_constraint(x, pltpu.HBM)
            for x in (teacher_feats, student_feats, prototypes)
        ],
        scratch=(half, half, pltpu.SemaphoreType.DMA((3 + NZ,))),
        specs=[ANY] * 3,
        out_specs=(ANY, VMEM, VMEM),
    )
    teach = lax.all_to_all(teach, "z", 0, 0, tiled=True)
    got = lax.ppermute(stud, "z", [(i, i ^ 4) for i in range(NZ)])
    far = [shift(proto, "core", NC, 1) for proto in near]

    col_shape = struct((TGROUP, PROWS, LANES), F32)
    row_shape = struct((PGROUP, TROWS, LANES), BF16)
    weights = pltpu.VMEM((PROWS, LANES), F32)

    square = pltpu.VMEM((HALF, TOK), F32)
    unit_shape = struct((HALF, K), BF16)
    half_sums = pltpu.VMEM((HROWS, LANES), F32)
    near_expo, near, far_expo, far, cols = call(
        both_teacher_kernel,
        (square, unit_shape, square, unit_shape, col_shape),
        teach,
        *near,
        *far,
        scratch=(half_sums, half_sums),
    )
    pieces = [stud, got]
    for step in range(ITERS):
        if step + 1 < ITERS:
            cols, pieces = lax.optimization_barrier((cols, pieces))
            held = jnp.concatenate(pieces, axis=0)
            cols, held = lax.optimization_barrier((cols, held))
            hop = (2, 1)[step]
            got = lax.ppermute(held, "z", [(i, i ^ hop) for i in range(NZ)])
        cols = lax.all_to_all(cols, ("y", "core"), 0, 0, tiled=True)
        if step + 1 < ITERS:
            pieces = pieces + [got]
            rows = call(
                row_kernel, row_shape, cols, pinned(near_expo), pinned(far_expo), scratch=(weights,)
            )
            rows = lax.all_to_all(rows, ("z", "x"), 0, 0, tiled=True)
            cols = call(col_kernel, col_shape, rows, pinned(near_expo), pinned(far_expo))
    near_expz, far_expz, stud, rows = call(
        last_row_kernel,
        (
            square,
            square,
            struct((TOK, K), BF16),
            struct((PGROUP, 2 * TROWS, LANES), BF16),
        ),
        *pieces,
        cols,
        near,
        far,
        pinned(near_expo),
        pinned(far_expo),
        scratch=(weights,),
    )
    rows = lax.all_to_all(rows, ("z", "x"), 0, 0, tiled=True)

    def grad(*tasks, after=()):
        sums, _ = lax.optimization_barrier((rows, after))
        return call(
            functools.partial(grad_kernel, tasks),
            (struct((PRO_BLOCK, K), F32),) * len(tasks),
            cols,
            sums,
            stud,
            *[pinned(x) for x in (near_expo, far_expo, near_expz, far_expz)],
            scratch=(weights,),
        )

    def swap(part):
        return shift(part, "core", NC, 1)

    def merge(near, far):
        return (near + swap(far)).astype(BF16)

    (far2,) = grad((1, 2))
    near2, far1, far3 = grad((0, 2), (1, 1), (1, 3), after=far2)
    parts = [merge(near2, far2)]
    near1, near3, near0, far0 = grad((0, 1), (0, 3), (0, 0), (1, 0), after=parts)
    parts += [merge(near1, far1), merge(near3, far3)]
    total = near0 + swap(far0)
    for part, step in zip(parts, (2, 1, 3)):
        total = total + shift(part, "y", NY, step).astype(F32)
    return total


def solution(mesh):
    grid = Mesh(mesh.devices.reshape(NZ, NY, NX, NC), ("z", "y", "x", "core"))
    tokens = P(("z", "y"), None)
    protos = P(("z", "y", "x", "core"), None)
    return jax.shard_map(
        shards, mesh=grid, in_specs=(tokens, tokens, protos), out_specs=protos, check_vma=False
    )
```

```python
import functools
import math

import jax
import jax.numpy as jnp
from jax import lax
from jax.experimental import pallas as pl
from jax.experimental.pallas import tpu as pltpu
from jax.sharding import Mesh, PartitionSpec as P

K = 384
PROTO = 65536
TOKENS = 8192
ITERS = 3
TEMP_TEACHER = 0.07
TEMP_STUDENT = 0.1
LOG2E = math.log2(math.e)
SCALE = PROTO / (TEMP_STUDENT * math.sqrt(TOKENS))

NZ, NY, NX, NC = 8, 4, 4, 2
TOK_BLOCK = TOKENS // (NZ * NY)
TOK_HALF = TOK_BLOCK // NC
PRO_BLOCK = PROTO // (NZ * NY * NX * NC)
TOK = TOK_HALF * NZ
PRO = PRO_BLOCK * NY * NC
HALF = PRO // 2
LANES = 128
TROWS = TOK // LANES
PROWS = PRO // LANES
HROWS = HALF // LANES
TGROUP = NY * NC
PGROUP = NZ * NX

F32 = jnp.float32
BF16 = jnp.bfloat16
VMEM = pl.BlockSpec(memory_space=pltpu.VMEM)
ANY = pl.BlockSpec(memory_space=pl.ANY)
PARAMS = pltpu.CompilerParams(vmem_limit_bytes=24 * 1024 * 1024)
CONTRACT_LAST = (((1,), (1,)), ((), ()))


def pinned(x):
    return pltpu.with_memory_space_constraint(x, pltpu.VMEM)


def unit(values):
    wide = values.astype(F32)
    return (wide * lax.rsqrt(jnp.sum(wide * wide, axis=1, keepdims=True) + 1e-06)).astype(BF16)


def norm_kernel(teach_hbm, stud_hbm, proto_hbm, teach_out, stud_out, proto_out, teach_buf, stud_buf, sems):
    half = pl.ds(pl.multiple_of(lax.axis_index("core") * TOK_HALF, TOK_HALF), TOK_HALF)
    copies = [
        pltpu.make_async_copy(teach_hbm.at[half, :], teach_buf, sems.at[0]),
        pltpu.make_async_copy(stud_hbm.at[half, :], stud_buf, sems.at[1]),
        pltpu.make_async_copy(proto_hbm, proto_out, sems.at[2]),
    ]
    for copy in copies:
        copy.start()
    copies[0].wait()
    teach_buf[...] = unit(teach_buf[...])
    spread = [pltpu.make_async_copy(teach_buf, teach_out.at[z], sems.at[3 + z]) for z in range(NZ)]
    for copy in spread:
        copy.start()
    copies[1].wait()
    stud_out[...] = unit(stud_buf[...])
    copies[2].wait()
    for copy in spread:
        copy.wait()


def to_rows(values):
    return jnp.sum(values.T, axis=0, keepdims=True)


def to_cols(row):
    return jnp.broadcast_to(row, (LANES, LANES)).T


def own_first(core, which):
    return core if which == 0 else 1 - core


def block_row(step):
    place = lax.rem(lax.axis_index("y") + (NY - step), NY)
    return pl.multiple_of(place * PRO_BLOCK, PRO_BLOCK)


def teacher_kernel(teach_ref, *refs):
    raw, (expo_ref, unit_ref, sums_ref) = refs[:NY], refs[NY:]
    teach = teach_ref[...].reshape(TOK, K)
    for step in range(NY):
        base = block_row(step)
        rows = pl.ds(base, PRO_BLOCK)
        proto = unit(raw[step][...])
        unit_ref[rows, :] = proto
        logits = lax.dot_general(proto, teach, CONTRACT_LAST, preferred_element_type=F32)
        expo = jnp.exp2(logits * (LOG2E / TEMP_TEACHER))
        expo_ref[rows, :] = expo
        total = sum(expo[:, j * LANES : (j + 1) * LANES] for j in range(TROWS))
        for k in range(PRO_BLOCK // LANES):
            sums_ref[pl.ds(base // LANES + k, 1), :] = to_rows(total[k * LANES : (k + 1) * LANES, :])


def both_teacher_kernel(teach_ref, *refs):
    near, far, outs = refs[:NY], refs[NY : 2 * NY], refs[2 * NY :]
    near_ref, near_unit, far_ref, far_unit, sums_ref, near_sums, far_sums, all_ref = outs
    teacher_kernel(teach_ref, *near, near_ref, near_unit, near_sums)
    teacher_kernel(teach_ref, *far, far_ref, far_unit, far_sums)
    core = lax.axis_index("core")
    for which, part_ref in enumerate((near_sums, far_sums)):
        base = pl.multiple_of(own_first(core, which) * HROWS, HROWS)
        all_ref[pl.ds(base, HROWS), :] = part_ref[...]
    spread_sums(all_ref, sums_ref)


def spread_sums(all_ref, sums_ref):
    sums = all_ref[...].astype(sums_ref.dtype)
    for peer in range(TGROUP):
        sums_ref[peer] = sums


def col_kernel(row_sums_ref, first_ref, second_ref, sums_ref, all_ref):
    weights = 1.0 / jnp.sum(row_sums_ref[...].astype(F32), axis=0)
    core = lax.axis_index("core")
    for which, expo_ref in enumerate((first_ref, second_ref)):
        base = own_first(core, which) * HROWS
        for i in range(HROWS):
            rows = slice(i * LANES, (i + 1) * LANES)
            total = None
            for j in range(TROWS):
                term = expo_ref[rows, j * LANES : (j + 1) * LANES] * weights[j : j + 1, :]
                total = term if total is None else total + term
            all_ref[pl.ds(base + i, 1), :] = to_rows(total)
    spread_sums(all_ref, sums_ref)


def row_sums(expo_refs, weights_ref):
    core = lax.axis_index("core")
    totals = (jnp.zeros((8, LANES), F32),) * TROWS
    for which, expo_ref in enumerate(expo_refs):
        base = own_first(core, which) * HROWS

        def group(i, totals):
            rows = pl.ds(pl.multiple_of(i * LANES, LANES), LANES)
            wide = to_cols(weights_ref[pl.ds(base + i, 1), :])
            out = []
            for j in range(TROWS):
                term = expo_ref[rows, j * LANES : (j + 1) * LANES] * wide
                out.append(totals[j] + jnp.sum(term.reshape(LANES // 8, 8, LANES), axis=0))
            return tuple(out)

        totals = lax.fori_loop(0, HROWS, group, totals, unroll=True)
    return jnp.concatenate([jnp.sum(t, axis=0, keepdims=True) for t in totals], axis=0)


def row_kernel(col_sums_ref, first_ref, second_ref, sums_ref, weights_ref):
    weights_ref[...] = 1.0 / jnp.sum(col_sums_ref[...].astype(F32), axis=0)
    sums = row_sums((first_ref, second_ref), weights_ref).astype(BF16)
    for peer in range(PGROUP):
        sums_ref[peer] = sums


def last_row_kernel(*refs):
    pieces, (col_sums_ref, *protos), expos, outs = refs[:4], refs[4:7], refs[7:9], refs[9:]
    *expzs, stud_out, sums_ref, weights_ref = outs
    place = lax.axis_index("z")
    offsets = [0]
    for piece, hop in zip(pieces, (0, 4, 2, 1)):
        hops = [o ^ hop for o in offsets]
        for i, hop_to in enumerate(hops):
            rows = pl.ds(pl.multiple_of((place ^ hop_to) * TOK_HALF, TOK_HALF), TOK_HALF)
            stud_out[rows, :] = piece[i * TOK_HALF : (i + 1) * TOK_HALF, :]
        if hop:
            offsets = offsets + hops
    stud = stud_out[...]
    weights_ref[...] = 1.0 / jnp.sum(col_sums_ref[...].astype(F32), axis=0)
    totals = [jnp.zeros((8, LANES), F32)] * TROWS
    for i in range(PRO // PRO_BLOCK):
        proto_ref, expz_ref = protos[i // NY], expzs[i // NY]
        rows = slice(i % NY * PRO_BLOCK, (i % NY + 1) * PRO_BLOCK)
        logits = lax.dot_general(
            proto_ref[rows, :], stud, CONTRACT_LAST, preferred_element_type=F32
        )
        expz = jnp.exp2(logits * (LOG2E / TEMP_STUDENT))
        expz_ref[rows, :] = expz
        for j in range(TROWS):
            part = expz[:, j * LANES : (j + 1) * LANES]
            totals[j] = totals[j] + jnp.sum(part.reshape(PRO_BLOCK // 8, 8, LANES), axis=0)
    stud_sums = [jnp.sum(t, axis=0, keepdims=True) for t in totals]
    sums = jnp.concatenate([row_sums(expos, weights_ref)] + stud_sums, axis=0).astype(BF16)
    for peer in range(PGROUP):
        sums_ref[peer] = sums


def grad_kernel(tasks, col_sums_ref, row_sums_ref, stud_ref, *refs):
    expos, expzs, outs, weights_ref = refs[:2], refs[2:4], refs[4:-1], refs[-1]
    core = lax.axis_index("core")
    weights_ref[...] = 1.0 / jnp.sum(col_sums_ref[...].astype(F32), axis=0)
    totals = jnp.sum(row_sums_ref[...].astype(F32), axis=0)
    target_scale = SCALE / totals[:TROWS]
    prob_scale = SCALE / totals[TROWS:]
    stud = stud_ref[...]
    for (which, step), out_ref in zip(tasks, outs):
        expo_ref, expz_ref = expos[which], expzs[which]
        base = own_first(core, which) * HROWS
        group = lax.rem(lax.axis_index("y") + step, NY) * (PRO_BLOCK // LANES)
        parts = []
        for k in range(PRO_BLOCK // LANES):
            wide = to_cols(weights_ref[pl.ds(base + group + k, 1), :])
            rows = pl.ds(pl.multiple_of((group + k) * LANES, LANES), LANES)
            cols = []
            for j in range(TROWS):
                lanes = slice(j * LANES, (j + 1) * LANES)
                target = (expo_ref[rows, lanes] * wide) * target_scale[j : j + 1, :]
                prob = expz_ref[rows, lanes] * prob_scale[j : j + 1, :]
                cols.append((prob - target).astype(BF16))
            parts.append(jnp.concatenate(cols, axis=1))
        grads = jnp.concatenate(parts, axis=0)
        out_ref[...] = jnp.dot(grads, stud, preferred_element_type=F32)


def call(kernel, out_shape, *args, scratch=(), specs=None, out_specs=None):
    return pl.pallas_call(
        kernel,
        out_shape=out_shape,
        in_specs=specs or [VMEM] * len(args),
        out_specs=out_specs or jax.tree.map(lambda _: VMEM, out_shape),
        scratch_shapes=scratch,
        compiler_params=PARAMS,
    )(*args)


def shift(x, axis, size, step):
    return lax.ppermute(x, axis, [(i, (i + step) % size) for i in range(size)])


def shards(teacher_feats, student_feats, prototypes):
    struct = jax.ShapeDtypeStruct
    near = [prototypes] + [shift(prototypes, "y", NY, step) for step in range(1, NY)]
    half = pltpu.VMEM((TOK_HALF, K), BF16)
    teach, stud, near[0] = call(
        norm_kernel,
        (
            struct((NZ, TOK_HALF, K), BF16),
            struct((TOK_HALF, K), BF16),
            struct((PRO_BLOCK, K), BF16),
        ),
        *[
            pltpu.with_memory_space_constraint(x, pltpu.HBM)
            for x in (teacher_feats, student_feats, prototypes)
        ],
        scratch=(half, half, pltpu.SemaphoreType.DMA((3 + NZ,))),
        specs=[ANY] * 3,
        out_specs=(ANY, VMEM, VMEM),
    )
    teach = lax.all_to_all(teach, "z", 0, 0, tiled=True)
    got = lax.ppermute(stud, "z", [(i, i ^ 4) for i in range(NZ)])
    far = [shift(proto, "core", NC, 1) for proto in near]

    col_shape = struct((TGROUP, PROWS, LANES), BF16)
    last_col_shape = struct((TGROUP, PROWS, LANES), F32)
    row_shape = struct((PGROUP, TROWS, LANES), BF16)
    weights = pltpu.VMEM((PROWS, LANES), F32)

    square = pltpu.VMEM((HALF, TOK), F32)
    unit_shape = struct((HALF, K), BF16)
    half_sums = pltpu.VMEM((HROWS, LANES), F32)
    near_expo, near, far_expo, far, cols = call(
        both_teacher_kernel,
        (square, unit_shape, square, unit_shape, col_shape),
        teach,
        *near,
        *far,
        scratch=(half_sums, half_sums, weights),
    )
    pieces = [stud, got]
    for step in range(ITERS):
        if step + 1 < ITERS:
            cols, pieces = lax.optimization_barrier((cols, pieces))
            held = jnp.concatenate(pieces, axis=0)
            cols, held = lax.optimization_barrier((cols, held))
            hop = (2, 1)[step]
            got = lax.ppermute(held, "z", [(i, i ^ hop) for i in range(NZ)])
        cols = lax.all_to_all(cols, ("y", "core"), 0, 0, tiled=True)
        if step + 1 < ITERS:
            pieces = pieces + [got]
            rows = call(
                row_kernel, row_shape, cols, pinned(near_expo), pinned(far_expo), scratch=(weights,)
            )
            rows = lax.all_to_all(rows, ("z", "x"), 0, 0, tiled=True)
            cols = call(
                col_kernel,
                last_col_shape if step + 2 == ITERS else col_shape,
                rows,
                pinned(near_expo),
                pinned(far_expo),
                scratch=(weights,),
            )
    near_expz, far_expz, stud, rows = call(
        last_row_kernel,
        (
            square,
            square,
            struct((TOK, K), BF16),
            struct((PGROUP, 2 * TROWS, LANES), BF16),
        ),
        *pieces,
        cols,
        near,
        far,
        pinned(near_expo),
        pinned(far_expo),
        scratch=(weights,),
    )
    rows = lax.all_to_all(rows, ("z", "x"), 0, 0, tiled=True)

    def grad(*tasks, after=()):
        sums, _ = lax.optimization_barrier((rows, after))
        return call(
            functools.partial(grad_kernel, tasks),
            (struct((PRO_BLOCK, K), F32),) * len(tasks),
            cols,
            sums,
            stud,
            *[pinned(x) for x in (near_expo, far_expo, near_expz, far_expz)],
            scratch=(weights,),
        )

    def swap(part):
        return shift(part, "core", NC, 1)

    def merge(near, far):
        return (near + swap(far)).astype(BF16)

    (far2,) = grad((1, 2))
    near2, far1, far3 = grad((0, 2), (1, 1), (1, 3), after=far2)
    parts = [merge(near2, far2)]
    near1, near3, near0, far0 = grad((0, 1), (0, 3), (0, 0), (1, 0), after=parts)
    parts += [merge(near1, far1), merge(near3, far3)]
    total = near0 + swap(far0)
    for part, step in zip(parts, (2, 1, 3)):
        total = total + shift(part, "y", NY, step).astype(F32)
    return total


def solution(mesh):
    grid = Mesh(mesh.devices.reshape(NZ, NY, NX, NC), ("z", "y", "x", "core"))
    tokens = P(("z", "y"), None)
    protos = P(("z", "y", "x", "core"), None)
    return jax.shard_map(
        shards, mesh=grid, in_specs=(tokens, tokens, protos), out_specs=protos, check_vma=False
    )
```

```python
import functools
import math

import jax
import jax.numpy as jnp
from jax import lax
from jax.experimental import pallas as pl
from jax.experimental.pallas import tpu as pltpu
from jax.sharding import Mesh, PartitionSpec as P

K = 384
PROTO = 65536
TOKENS = 8192
ITERS = 3
TEMP_TEACHER = 0.07
TEMP_STUDENT = 0.1
LOG2E = math.log2(math.e)
SCALE = PROTO / (TEMP_STUDENT * math.sqrt(TOKENS))

NZ, NY, NX, NC = 8, 4, 4, 2
TOK_BLOCK = TOKENS // (NZ * NY)
TOK_HALF = TOK_BLOCK // NC
PRO_BLOCK = PROTO // (NZ * NY * NX * NC)
TOK = TOK_HALF * NZ
PRO = PRO_BLOCK * NY * NC
HALF = PRO // 2
LANES = 128
TROWS = TOK // LANES
PROWS = PRO // LANES
HROWS = HALF // LANES
TGROUP = NY * NC
PGROUP = NZ * NX

F32 = jnp.float32
BF16 = jnp.bfloat16
VMEM = pl.BlockSpec(memory_space=pltpu.VMEM)
ANY = pl.BlockSpec(memory_space=pl.ANY)
PARAMS = pltpu.CompilerParams(vmem_limit_bytes=24 * 1024 * 1024)
CONTRACT_LAST = (((1,), (1,)), ((), ()))


def pinned(x):
    return pltpu.with_memory_space_constraint(x, pltpu.VMEM)


def unit(values):
    wide = values.astype(F32)
    return (wide * lax.rsqrt(jnp.sum(wide * wide, axis=1, keepdims=True) + 1e-06)).astype(BF16)


def norm_kernel(teach_hbm, stud_hbm, proto_hbm, teach_out, stud_out, proto_out, teach_buf, stud_buf, sems):
    half = pl.ds(pl.multiple_of(lax.axis_index("core") * TOK_HALF, TOK_HALF), TOK_HALF)
    copies = [
        pltpu.make_async_copy(teach_hbm.at[half, :], teach_buf, sems.at[0]),
        pltpu.make_async_copy(stud_hbm.at[half, :], stud_buf, sems.at[1]),
        pltpu.make_async_copy(proto_hbm, proto_out, sems.at[2]),
    ]
    for copy in copies:
        copy.start()
    copies[0].wait()
    teach_buf[...] = unit(teach_buf[...])
    spread = [pltpu.make_async_copy(teach_buf, teach_out.at[z], sems.at[3 + z]) for z in range(NZ)]
    for copy in spread:
        copy.start()
    copies[1].wait()
    stud_out[...] = unit(stud_buf[...])
    copies[2].wait()
    for copy in spread:
        copy.wait()


def to_rows(values):
    return jnp.sum(values.T, axis=0, keepdims=True)


def to_cols(row):
    return jnp.broadcast_to(row, (LANES, LANES)).T


def own_first(core, which):
    return core if which == 0 else 1 - core


def block_row(step):
    place = lax.rem(lax.axis_index("y") + (NY - step), NY)
    return pl.multiple_of(place * PRO_BLOCK, PRO_BLOCK)


def teacher_kernel(teach_ref, *refs):
    raw, (expo_ref, unit_ref, sums_ref) = refs[:NY], refs[NY:]
    teach = teach_ref[...].reshape(TOK, K)
    for step in range(NY):
        base = block_row(step)
        rows = pl.ds(base, PRO_BLOCK)
        proto = unit(raw[step][...])
        unit_ref[rows, :] = proto
        logits = lax.dot_general(proto, teach, CONTRACT_LAST, preferred_element_type=F32)
        expo = jnp.exp2(logits * (LOG2E / TEMP_TEACHER))
        expo_ref[rows, :] = expo
        total = sum(expo[:, j * LANES : (j + 1) * LANES] for j in range(TROWS))
        for k in range(PRO_BLOCK // LANES):
            sums_ref[pl.ds(base // LANES + k, 1), :] = to_rows(total[k * LANES : (k + 1) * LANES, :])


def both_teacher_kernel(teach_ref, *refs):
    near, far, outs = refs[:NY], refs[NY : 2 * NY], refs[2 * NY :]
    near_ref, near_unit, far_ref, far_unit, sums_ref, near_sums, far_sums, all_ref = outs
    teacher_kernel(teach_ref, *near, near_ref, near_unit, near_sums)
    teacher_kernel(teach_ref, *far, far_ref, far_unit, far_sums)
    core = lax.axis_index("core")
    for which, part_ref in enumerate((near_sums, far_sums)):
        base = pl.multiple_of(own_first(core, which) * HROWS, HROWS)
        all_ref[pl.ds(base, HROWS), :] = part_ref[...]
    spread_sums(all_ref, sums_ref)


def spread_sums(all_ref, sums_ref):
    sums = all_ref[...].astype(sums_ref.dtype)
    for peer in range(TGROUP):
        sums_ref[peer] = sums


def col_kernel(row_sums_ref, first_ref, second_ref, sums_ref, all_ref):
    weights = 1.0 / jnp.sum(row_sums_ref[...].astype(F32), axis=0)
    core = lax.axis_index("core")
    for which, expo_ref in enumerate((first_ref, second_ref)):
        base = own_first(core, which) * HROWS
        for i in range(HROWS):
            rows = slice(i * LANES, (i + 1) * LANES)
            total = None
            for j in range(TROWS):
                term = expo_ref[rows, j * LANES : (j + 1) * LANES] * weights[j : j + 1, :]
                total = term if total is None else total + term
            all_ref[pl.ds(base + i, 1), :] = to_rows(total)
    spread_sums(all_ref, sums_ref)


def row_sums(expo_refs, weights_ref):
    core = lax.axis_index("core")
    totals = (jnp.zeros((8, LANES), F32),) * TROWS
    for which, expo_ref in enumerate(expo_refs):
        base = own_first(core, which) * HROWS

        def group(i, totals):
            rows = pl.ds(pl.multiple_of(i * LANES, LANES), LANES)
            wide = to_cols(weights_ref[pl.ds(base + i, 1), :])
            out = []
            for j in range(TROWS):
                term = expo_ref[rows, j * LANES : (j + 1) * LANES] * wide
                out.append(totals[j] + jnp.sum(term.reshape(LANES // 8, 8, LANES), axis=0))
            return tuple(out)

        totals = lax.fori_loop(0, HROWS, group, totals, unroll=True)
    return jnp.concatenate([jnp.sum(t, axis=0, keepdims=True) for t in totals], axis=0)


def row_kernel(col_sums_ref, first_ref, second_ref, sums_ref, weights_ref):
    weights_ref[...] = 1.0 / jnp.sum(col_sums_ref[...].astype(F32), axis=0)
    sums = row_sums((first_ref, second_ref), weights_ref).astype(BF16)
    for peer in range(PGROUP):
        sums_ref[peer] = sums


def last_row_kernel(*refs):
    pieces, (col_sums_ref, *protos), expos, outs = refs[:4], refs[4:7], refs[7:9], refs[9:]
    *expzs, stud_out, sums_ref, weights_ref = outs
    place = lax.axis_index("z")
    offsets = [0]
    for piece, hop in zip(pieces, (0, 4, 2, 1)):
        hops = [o ^ hop for o in offsets]
        for i, hop_to in enumerate(hops):
            rows = pl.ds(pl.multiple_of((place ^ hop_to) * TOK_HALF, TOK_HALF), TOK_HALF)
            stud_out[rows, :] = piece[i * TOK_HALF : (i + 1) * TOK_HALF, :]
        if hop:
            offsets = offsets + hops
    stud = stud_out[...]
    weights_ref[...] = 1.0 / jnp.sum(col_sums_ref[...].astype(F32), axis=0)
    totals = [jnp.zeros((8, LANES), F32)] * TROWS
    for i in range(PRO // PRO_BLOCK):
        proto_ref, expz_ref = protos[i // NY], expzs[i // NY]
        rows = slice(i % NY * PRO_BLOCK, (i % NY + 1) * PRO_BLOCK)
        logits = lax.dot_general(
            proto_ref[rows, :], stud, CONTRACT_LAST, preferred_element_type=F32
        )
        expz = jnp.exp2(logits * (LOG2E / TEMP_STUDENT))
        expz_ref[rows, :] = expz
        for j in range(TROWS):
            part = expz[:, j * LANES : (j + 1) * LANES]
            totals[j] = totals[j] + jnp.sum(part.reshape(PRO_BLOCK // 8, 8, LANES), axis=0)
    stud_sums = [jnp.sum(t, axis=0, keepdims=True) for t in totals]
    sums = jnp.concatenate([row_sums(expos, weights_ref)] + stud_sums, axis=0).astype(BF16)
    for peer in range(PGROUP):
        sums_ref[peer] = sums


def grad_kernel(tasks, col_sums_ref, row_sums_ref, stud_ref, *refs):
    expos, expzs, outs, weights_ref = refs[:2], refs[2:4], refs[4:-1], refs[-1]
    core = lax.axis_index("core")
    weights_ref[...] = 1.0 / jnp.sum(col_sums_ref[...].astype(F32), axis=0)
    totals = jnp.sum(row_sums_ref[...].astype(F32), axis=0)
    target_scale = SCALE / totals[:TROWS]
    prob_scale = SCALE / totals[TROWS:]
    stud = stud_ref[...]
    for (which, step), out_ref in zip(tasks, outs):
        expo_ref, expz_ref = expos[which], expzs[which]
        base = own_first(core, which) * HROWS
        group = lax.rem(lax.axis_index("y") + step, NY) * (PRO_BLOCK // LANES)
        parts = []
        for k in range(PRO_BLOCK // LANES):
            wide = to_cols(weights_ref[pl.ds(base + group + k, 1), :])
            rows = pl.ds(pl.multiple_of((group + k) * LANES, LANES), LANES)
            cols = []
            for j in range(TROWS):
                lanes = slice(j * LANES, (j + 1) * LANES)
                target = (expo_ref[rows, lanes] * wide) * target_scale[j : j + 1, :]
                prob = expz_ref[rows, lanes] * prob_scale[j : j + 1, :]
                cols.append((prob - target).astype(BF16))
            parts.append(jnp.concatenate(cols, axis=1))
        grads = jnp.concatenate(parts, axis=0)
        out_ref[...] = jnp.dot(grads, stud, preferred_element_type=F32)


def call(kernel, out_shape, *args, scratch=(), specs=None, out_specs=None):
    return pl.pallas_call(
        kernel,
        out_shape=out_shape,
        in_specs=specs or [VMEM] * len(args),
        out_specs=out_specs or jax.tree.map(lambda _: VMEM, out_shape),
        scratch_shapes=scratch,
        compiler_params=PARAMS,
    )(*args)


def shift(x, axis, size, step):
    return lax.ppermute(x, axis, [(i, (i + step) % size) for i in range(size)])


def shards(teacher_feats, student_feats, prototypes):
    struct = jax.ShapeDtypeStruct
    near = [prototypes] + [shift(prototypes, "y", NY, step) for step in range(1, NY)]
    half = pltpu.VMEM((TOK_HALF, K), BF16)
    teach, stud, near[0] = call(
        norm_kernel,
        (
            struct((NZ, TOK_HALF, K), BF16),
            struct((TOK_HALF, K), BF16),
            struct((PRO_BLOCK, K), BF16),
        ),
        *[
            pltpu.with_memory_space_constraint(x, pltpu.HBM)
            for x in (teacher_feats, student_feats, prototypes)
        ],
        scratch=(half, half, pltpu.SemaphoreType.DMA((3 + NZ,))),
        specs=[ANY] * 3,
        out_specs=(ANY, VMEM, VMEM),
    )
    teach = lax.all_to_all(teach, "z", 0, 0, tiled=True)
    got = lax.ppermute(stud, "z", [(i, i ^ 4) for i in range(NZ)])
    far = [shift(proto, "core", NC, 1) for proto in near]

    col_shape = struct((TGROUP, PROWS, LANES), BF16)
    last_col_shape = struct((TGROUP, PROWS, LANES), F32)
    row_shape = struct((PGROUP, TROWS, LANES), BF16)
    weights = pltpu.VMEM((PROWS, LANES), F32)

    square = pltpu.VMEM((HALF, TOK), F32)
    unit_shape = struct((HALF, K), BF16)
    half_sums = pltpu.VMEM((HROWS, LANES), F32)
    near_expo, near, far_expo, far, cols = call(
        both_teacher_kernel,
        (square, unit_shape, square, unit_shape, col_shape),
        teach,
        *near,
        *far,
        scratch=(half_sums, half_sums, weights),
    )
    pieces = [stud, got]
    for step in range(ITERS):
        if step + 1 < ITERS:
            cols, pieces = lax.optimization_barrier((cols, pieces))
            held = jnp.concatenate(pieces, axis=0)
            cols, held = lax.optimization_barrier((cols, held))
            hop = (2, 1)[step]
            got = lax.ppermute(held, "z", [(i, i ^ hop) for i in range(NZ)])
        cols = lax.all_to_all(cols, ("y", "core"), 0, 0, tiled=True)
        if step + 1 < ITERS:
            pieces = pieces + [got]
            rows = call(
                row_kernel, row_shape, cols, pinned(near_expo), pinned(far_expo), scratch=(weights,)
            )
            rows = lax.all_to_all(rows, ("z", "x"), 0, 0, tiled=True)
            cols = call(
                col_kernel,
                last_col_shape if step + 2 == ITERS else col_shape,
                rows,
                pinned(near_expo),
                pinned(far_expo),
                scratch=(weights,),
            )
    near_expz, far_expz, stud, rows = call(
        last_row_kernel,
        (
            square,
            square,
            struct((TOK, K), BF16),
            struct((PGROUP, 2 * TROWS, LANES), BF16),
        ),
        *pieces,
        cols,
        near,
        far,
        pinned(near_expo),
        pinned(far_expo),
        scratch=(weights,),
    )
    rows = lax.all_to_all(rows, ("z", "x"), 0, 0, tiled=True)

    def grad(*tasks, after=()):
        sums, _ = lax.optimization_barrier((rows, after))
        return call(
            functools.partial(grad_kernel, tasks),
            (struct((PRO_BLOCK, K), F32),) * len(tasks),
            cols,
            sums,
            stud,
            *[pinned(x) for x in (near_expo, far_expo, near_expz, far_expz)],
            scratch=(weights,),
        )

    def swap(part):
        return shift(part, "core", NC, 1)

    def merge(near, far):
        return (near + swap(far)).astype(BF16)

    far2, near2 = grad((1, 2), (0, 2))
    far1, far3 = grad((1, 1), (1, 3), after=far2)
    parts = [merge(near2, far2)]
    near1, near3, near0, far0 = grad((0, 1), (0, 3), (0, 0), (1, 0), after=parts)
    parts += [merge(near1, far1), merge(near3, far3)]
    total = near0 + swap(far0)
    for part, step in zip(parts, (2, 1, 3)):
        total = total + shift(part, "y", NY, step).astype(F32)
    return total


def solution(mesh):
    grid = Mesh(mesh.devices.reshape(NZ, NY, NX, NC), ("z", "y", "x", "core"))
    tokens = P(("z", "y"), None)
    protos = P(("z", "y", "x", "core"), None)
    return jax.shard_map(
        shards, mesh=grid, in_specs=(tokens, tokens, protos), out_specs=protos, check_vma=False
    )
```
